128 devices in a mesh: ord: 16 (over z, y), lev: 8 (over x, core).
Axes of the slice: x: 4, y: 4, z: 4, core: 2. Of those that a mesh axis runs over, the one named last changes fastest.
Arguments:
- grid_grad: bfloat16 [1280, 136, 2560], P('ord', 'lev'), may hold values from -0.119628906 to 0.119628906
- legendre: bfloat16 [512, 1280, 1280], P(('ord', 'lev')), may hold values from -0.15625 to 0.15625
- cov_root: bfloat16 [1280, 136, 136], P('lev'), may hold values from -0.5 to 0.5
- order_ids: int32 [512], replicated, may hold values from 0 to 1279, as said below
- cycle_map: int32 [1280], replicated, may hold values from 0 to 1279, each once
Outputs:
- control_grad: float32 [1280, 512, 2, 136], P('lev', 'ord')
The draws below stay inside these ranges and needn't reach their ends.
Inputs may be any that keep to these rules, and one draw needn't show every extreme that they name: `order_ids`: distinct orders; 0 and 1279 are always among them. `cycle_map`: a permutation of the cycles.
All inputs are finite; a program needn't handle non-finite values.
Results may differ from the reference program's by a relative error of at most 0.0047.
Values may be sent and summed in bfloat16 or wider, within the bound.
No kernel may reach another device: no remote copies, remote signals or barrier semaphores. Data moves between devices by JAX's collectives and lax.ppermute only.
A program may use at most 128 MiB of HBM per device.

```python
import math
import jax
import jax.numpy as jnp
from jax import lax

NLON = 2560
NLAT = 1280
NDEG = 1280
LEV = 136
ORDERS = 512


def draw_order_ids(key, part):
    key = jax.random.fold_in(key, 7)
    first_key, second_key = jax.random.split(key)
    half_count = NDEG // 2
    others = jax.random.permutation(first_key, jnp.arange(1, half_count, dtype=jnp.int32))[:ORDERS // 2 - 1]
    lower = jnp.concatenate([jnp.zeros((1,), jnp.int32), others])
    lower = jax.random.permutation(second_key, lower)
    upper = NDEG - 1 - lower
    return jnp.stack([lower, upper], axis=1).reshape(ORDERS).astype(jnp.int32)


def shard_levels(own_key, shape, pieces, low, largest):
    gain, own = 1.0, jax.random.fold_in(own_key, 6)
    for dim, parts in pieces:
        draws = jnp.exp(jax.random.uniform(jax.random.fold_in(own, dim), (parts,), jnp.float32, low / len(pieces), largest / len(pieces)))
        gain = gain * jnp.repeat(draws, shape[dim] // parts).reshape([-1 if axis == dim else 1 for axis in range(len(shape))])
    return gain


def gaussian(stream_key, extent, spread, reach, pieces=(), held_as=jnp.bfloat16):
    drawn = jax.random.normal(stream_key, extent, jnp.float32) * spread
    if len(pieces) > 0:
        drawn = shard_levels(stream_key, extent, pieces, -0.22, 0.18) * drawn
    return jnp.clip(drawn, min=-reach, max=reach).astype(held_as)


def setup_inputs(seed: int = 0) -> dict:
    key_of = jax.random.split(jax.random.key(seed), 6)
    return {
        "grid_grad": gaussian(key_of[0], (NLAT, LEV, NLON), 0.02, 0.119628906, ((0, 16), (1, 8))),
        "legendre": gaussian(key_of[1], (ORDERS, NDEG, NLAT), NLAT ** -0.5, 0.15625, ((0, 128),)),
        "cov_root": gaussian(key_of[2], (NDEG, LEV, LEV), LEV ** -0.5, 0.5, ((0, 8),)),
        "order_ids": draw_order_ids(jax.random.fold_in(key_of[5], 71), 0),
        "cycle_map": jax.random.permutation(key_of[4], NLAT).astype(jnp.int32),
    }


def fourier_weights(order_ids, lon_count):
    longitudes = jnp.arange(lon_count, dtype=jnp.int32)
    phases = (longitudes[:, None] * order_ids[None, :].astype(jnp.int32)) % lon_count
    angles = phases.astype(jnp.float32) * (2.0 * math.pi / lon_count)
    scales = jnp.where(order_ids == 0, 1.0, 2.0).astype(jnp.float32)
    cosine = scales[None, :] * jnp.cos(angles)
    sine = -scales[None, :] * jnp.sin(angles)
    return jnp.stack([cosine, sine], axis=1).astype(jnp.bfloat16)


def reference(grid_grad, legendre, cov_root, order_ids, cycle_map):
    fourier_table = fourier_weights(order_ids, NLON)
    folded = jnp.dot(grid_grad.reshape(NLAT * LEV, NLON), fourier_table.reshape(NLON, 2 * ORDERS), preferred_element_type=jnp.float32)
    fourier = folded.reshape(NLAT, LEV, 2, ORDERS).transpose(3, 2, 1, 0).astype(jnp.bfloat16)
    degrees = jnp.arange(NDEG, dtype=jnp.int32)
    keep = degrees[None, :, None] >= order_ids.astype(jnp.int32)[:, None, None]
    masked_legendre = jnp.where(keep, legendre, jnp.zeros_like(legendre))

    def per_order(pair):
        table_row, spectrum = pair
        weights = jnp.take(table_row, cycle_map.astype(jnp.int32), axis=1)
        return jnp.dot(weights, spectrum.reshape(2 * LEV, NLAT).T, preferred_element_type=jnp.float32).astype(jnp.bfloat16)

    coefficients = lax.map(per_order, (masked_legendre, fourier))
    spectral = coefficients.reshape(ORDERS, NDEG, 2, LEV).astype(jnp.float32)
    return jnp.einsum("mncl,nlk->nmck", spectral, cov_root.astype(jnp.float32))
```

```python
import functools
import math

import jax
import jax.numpy as jnp
from jax import lax
from jax.experimental import pallas as pl
from jax.experimental.pallas import tpu as pltpu
from jax.sharding import PartitionSpec as P

MIB = 1024 * 1024
NT = (((1,), (1,)), ((), ()))


def unit_circle(phase, lon_count):
    quarter = lon_count // 4
    turns = jnp.floor(phase * (1.0 / quarter) + 0.5)
    angle = (phase - turns * quarter) * (2.0 * math.pi / lon_count)
    square = angle * angle
    sine = angle * (1.0 + square * (-1.0 / 6 + square * (1.0 / 120 + square * (-1.0 / 5040 + square * (1.0 / 362880)))))
    cosine = 1.0 + square * (-0.5 + square * (1.0 / 24 + square * (-1.0 / 720 + square * (1.0 / 40320))))
    quadrant = turns.astype(jnp.int32) & 3
    swap = (quadrant & 1) == 1
    cos_part = jnp.where(swap, sine, cosine)
    sin_part = jnp.where(swap, cosine, sine)
    cos_out = jnp.where((quadrant == 1) | (quadrant == 2), -cos_part, cos_part)
    sin_out = jnp.where(quadrant >= 2, -sin_part, sin_part)
    return cos_out, sin_out


def fourier_kernel(ids_ref, grid_ref, out_ref, table):
    rows, lon_count = table.shape
    order = ids_ref[...]
    row = lax.broadcasted_iota(jnp.int32, (rows, 1), 0)
    lane = lax.broadcasted_iota(jnp.int32, (rows, 128), 1).astype(jnp.float32)
    offset = jnp.where((row & 1) == 1, lon_count // 4, 0).astype(jnp.float32)
    scale = jnp.where(order == 0.0, 1.0, 2.0)
    cos_far, sin_far = unit_circle(order * 128.0 * lane + offset, lon_count)
    cos_near, sin_near = unit_circle(order * lane, lon_count)
    cos_far, sin_far = cos_far * scale, sin_far * scale
    for a in range(lon_count // 128):
        part = cos_far[:, a:a + 1] * cos_near - sin_far[:, a:a + 1] * sin_near
        table[:, a * 128:(a + 1) * 128] = part.astype(jnp.bfloat16)
    spectra = lax.dot_general(table[...], grid_ref[...], NT, preferred_element_type=jnp.float32)
    out_ref[...] = spectra.reshape(out_ref.shape).astype(jnp.bfloat16)


def fourier(grid_rows, order_ids, dests):
    points, lon_count = grid_rows.shape
    rows = 2 * order_ids.shape[0]
    steps = 4
    per_dest = rows // dests
    ids = jnp.repeat(order_ids, 2)[:, None].astype(jnp.float32)
    return pl.pallas_call(
        fourier_kernel,
        grid=(steps,),
        in_specs=[
            pl.BlockSpec((rows // steps, 1), lambda s: (s, 0)),
            pl.BlockSpec((points, lon_count), lambda s: (0, 0)),
        ],
        out_specs=pl.BlockSpec((dests // steps, per_dest, points), lambda s: (s, 0, 0)),
        out_shape=jax.ShapeDtypeStruct((dests, per_dest, points), jnp.bfloat16),
        scratch_shapes=[pltpu.VMEM((rows // steps, lon_count), jnp.bfloat16)],
        compiler_params=pltpu.CompilerParams(vmem_limit_bytes=48 * MIB),
        name="fourier_analysis",
    )(ids, grid_rows)


def legendre_kernel(ids_ref, got_ref, perm_ref, leg_ref, out_ref, rows_x, rows_z, spectra, rest, *, ord_count, lev_count, lev_dev, cycles_dev, deg_block):
    step = pl.program_id(0)
    orders = leg_ref.shape[0]
    pairs = 2 * orders
    levels = lev_count * lev_dev

    @pl.when(step == 0)
    def _():
        def gather(g, carry):
            for t in range(lev_dev):
                halves = []
                for q in (2 * t, 2 * t + 1):
                    b, l = 2 * g + q // lev_dev, q % lev_dev
                    halves.append(jnp.concatenate([
                        got_ref[a * lev_count + b, :, l * cycles_dev:(l + 1) * cycles_dev].astype(jnp.float32)
                        for a in range(ord_count)
                    ], axis=1))
                both = jnp.concatenate(halves, axis=0).astype(jnp.bfloat16)
                start = pl.multiple_of((2 * g * lev_dev + 2 * t) * pairs, 2 * pairs)
                rows_x[pl.ds(start, 2 * pairs), :] = both
            return carry

        lax.fori_loop(0, lev_count // 2, gather, 0)
        chunk = rows_x.shape[0] // 4

        def permute(g, carry):
            start = pl.multiple_of(g * chunk, 16)
            placed = jnp.dot(rows_x[pl.ds(start, chunk), :], perm_ref[...], preferred_element_type=jnp.float32)
            for t in range(rows_z.shape[0]):
                rows_z[t, pl.ds(start, chunk), :] = placed[:, t * 128:(t + 1) * 128]
            return carry

        lax.fori_loop(0, 4, permute, 0)
        for j in range(orders):
            tails = []
            for c in range(2):
                part = jnp.concatenate([
                    rows_z[t, pl.ds(2 * j + c, levels, stride=pairs), :]
                    for t in range(rows_z.shape[0])], axis=1)
                spectra[j, c * 128:(c + 1) * 128, :] = part[:128].astype(jnp.bfloat16)
                tails.append(part[128:])
            spectra[j, 256:, :] = jnp.concatenate(tails, axis=0).astype(jnp.bfloat16)

    span = leg_ref.shape[1]
    for j in range(orders):
        order = ids_ref[j]
        degree = step * span + lax.broadcasted_iota(jnp.int32, (span, 1), 0)
        used = (step + 1) * span > order

        @pl.when(used)
        def _():
            product = lax.dot_general(leg_ref[j], spectra[j], NT, preferred_element_type=jnp.float32)
            product = jnp.where(degree >= order, product, 0.0)
            for d in range(span // deg_block):
                own = product[d * deg_block:(d + 1) * deg_block]
                for c in range(2):
                    at = (2 * j + c) * deg_block
                    out_ref[d, at:at + deg_block, :] = own[:, c * 128:(c + 1) * 128].astype(jnp.bfloat16)
            rest[j, :, 0:16] = product[:, 256:]

        @pl.when(jnp.logical_not(used))
        def _():
            for d in range(span // deg_block):
                at = 2 * j * deg_block
                out_ref[d, at:at + 2 * deg_block, :] = jnp.zeros((2 * deg_block, 128), jnp.bfloat16)
            rest[j, :, 0:16] = jnp.zeros((span, 16), jnp.float32)

    tail = jnp.concatenate([rest[j, :, 0:16] for j in range(orders)], axis=1)
    half = deg_block // 2
    for d in range(span // deg_block):
        first = tail[d * deg_block:d * deg_block + half]
        second = tail[d * deg_block + half:(d + 1) * deg_block]
        out_ref[d, pairs * deg_block:, :] = jnp.concatenate([first, second], axis=1).astype(jnp.bfloat16)


def legendre_sums(own_orders, arrived, perm, legendre, ord_count, lev_count, lev_dev, cycles_dev):
    orders, degrees, cycles = legendre.shape
    deg_block = degrees // lev_count
    per_step = 2
    steps = lev_count // per_step
    packed = (2 * orders) * deg_block + deg_block // 2
    rows = 2 * orders * lev_count * lev_dev
    kernel = functools.partial(
        legendre_kernel, ord_count=ord_count, lev_count=lev_count, lev_dev=lev_dev,
        cycles_dev=cycles_dev, deg_block=deg_block)
    return pl.pallas_call(
        kernel,
        grid_spec=pltpu.PrefetchScalarGridSpec(
            num_scalar_prefetch=1,
            grid=(steps,),
            in_specs=[
                pl.BlockSpec(arrived.shape, lambda s, ids: (0, 0, 0)),
                pl.BlockSpec(perm.shape, lambda s, ids: (0, 0)),
                pl.BlockSpec((orders, per_step * deg_block, cycles), lambda s, ids: (0, s, 0)),
            ],
            out_specs=pl.BlockSpec((per_step, packed, 128), lambda s, ids: (s, 0, 0)),
            scratch_shapes=[
                pltpu.VMEM((rows, cycles), jnp.bfloat16),
                pltpu.VMEM((cycles // 128, rows, 128), jnp.float32),
                pltpu.VMEM((orders, 2 * lev_count * lev_dev, cycles), jnp.bfloat16),
                pltpu.VMEM((orders, per_step * deg_block, 128), jnp.float32),
            ],
        ),
        out_shape=jax.ShapeDtypeStruct((lev_count, packed, 128), jnp.bfloat16),
        compiler_params=pltpu.CompilerParams(vmem_limit_bytes=56 * MIB),
        name="legendre_sums",
    )(own_orders, arrived, perm, legendre)


def covariance_kernel(got_ref, cov_hbm, out_ref, cov, main, rest, out_main, out_rest, sems):
    step = pl.program_id(0)
    sources = got_ref.shape[0]
    pairs = main.shape[0] // (sources * cov.shape[0])
    deg_block, levels, _ = cov.shape
    half = deg_block // 2
    pieces = sems.shape[0]
    piece = deg_block // pieces
    rows = sources * pairs

    def load(p):
        return pltpu.make_async_copy(cov_hbm.at[pl.ds(p * piece, piece)], cov.at[pl.ds(p * piece, piece)], sems.at[p])

    @pl.when(step == 0)
    def _():
        for p in range(pieces):
            load(p).start()

        def unpack(s, carry):
            tail = got_ref[s, pairs * deg_block:, :].astype(jnp.float32)
            for r in range(pairs):
                base = pl.multiple_of((s * pairs + r) * deg_block, 16)
                main[pl.ds(base, deg_block), :] = got_ref[s, r * deg_block:(r + 1) * deg_block, :].astype(jnp.float32)
                for h in range(2):
                    at = h * 64 + r * 8
                    moved = tail if at == 0 else pltpu.roll(tail, 128 - at, 1)
                    rest[pl.ds(base + h * half, half), :] = moved
            return carry

        lax.fori_loop(0, sources, unpack, 0)
        for p in range(pieces):
            load(p).wait()

            def multiply(i, carry):
                n = p * piece + i
                left = jnp.concatenate([
                    main[pl.ds(n, rows, stride=deg_block), :],
                    rest[pl.ds(n, rows, stride=deg_block), :]], axis=1)[:, :levels].astype(jnp.bfloat16)
                product = jnp.dot(left, cov[n], preferred_element_type=jnp.float32)
                out_main[pl.ds(n, rows, stride=deg_block), :] = product[:, :128]
                out_rest[pl.ds(n, rows, stride=deg_block), :] = product[:, 128:]
                return carry

            lax.fori_loop(0, piece, multiply, 0, unroll=4)

    for r in range(pairs):
        base = pl.multiple_of((step * pairs + r) * deg_block, 16)
        out_ref[r // 2, r % 2, 0:128, :] = out_main[pl.ds(base, deg_block), :].T
        out_ref[r // 2, r % 2, 128:, :] = out_rest[pl.ds(base, deg_block), :].T[:levels - 128]


def covariance(arrived, cov, orders):
    sources, packed, _ = arrived.shape
    deg_block, levels, wide = cov.shape
    order_block = orders // sources
    rows = 2 * orders * deg_block
    pieces = 10
    return pl.pallas_call(
        covariance_kernel,
        grid=(sources,),
        in_specs=[
            pl.BlockSpec(arrived.shape, lambda s: (0, 0, 0)),
            pl.BlockSpec(memory_space=pl.ANY),
        ],
        out_specs=pl.BlockSpec((order_block, 2, levels, deg_block), lambda s: (s, 0, 0, 0)),
        out_shape=jax.ShapeDtypeStruct((orders, 2, levels, deg_block), jnp.float32),
        scratch_shapes=[
            pltpu.VMEM((deg_block, levels, wide), jnp.bfloat16),
            pltpu.VMEM((rows, 128), jnp.float32),
            pltpu.VMEM((rows, 128), jnp.float32),
            pltpu.VMEM((rows, 128), jnp.float32),
            pltpu.VMEM((rows, 128), jnp.float32),
            pltpu.SemaphoreType.DMA((pieces,)),
        ],
        compiler_params=pltpu.CompilerParams(vmem_limit_bytes=56 * MIB),
        name="vertical_covariance",
    )(arrived, cov)


def shards(grid_grad, legendre, cov_root, order_ids, cycle_map):
    cycles_dev, lev_dev, lon_count = grid_grad.shape
    orders_dev, degree_count, cycle_total = legendre.shape
    ord_count = lax.axis_size("ord")
    lev_count = lax.axis_size("lev")
    dests = ord_count * lev_count
    grid_rows = grid_grad.transpose(1, 0, 2).reshape(lev_dev * cycles_dev, lon_count)
    spectra = fourier(grid_rows, order_ids, dests)
    arrived = lax.all_to_all(spectra, ("ord", "lev"), split_axis=0, concat_axis=0, tiled=True)
    position = lax.axis_index("ord") * lev_count + lax.axis_index("lev")
    own_orders = lax.dynamic_slice_in_dim(order_ids, position * orders_dev, orders_dev, 0)
    perm = (cycle_map[:, None] == jnp.arange(cycle_total, dtype=jnp.int32)[None, :]).astype(jnp.bfloat16)
    packed = legendre_sums(own_orders, arrived, perm, legendre, ord_count, lev_count, lev_dev, cycles_dev)
    swapped = lax.all_to_all(packed, "lev", split_axis=0, concat_axis=0, tiled=True)
    levels = lev_dev * lev_count
    cov = jnp.pad(cov_root, ((0, 0), (0, 0), (0, 256 - levels)))
    out = covariance(swapped, cov, orders_dev * lev_count)
    return out.transpose(3, 0, 1, 2)


def solution(mesh):
    return jax.shard_map(
        shards,
        mesh=mesh,
        in_specs=(
            P("ord", "lev", None),
            P(("ord", "lev"), None, None),
            P("lev", None, None),
            P(),
            P(),
        ),
        out_specs=P("lev", "ord", None, None),
        check_vma=False,
    )
```

```python
import functools
import math

import jax
import jax.numpy as jnp
from jax import lax
from jax.experimental import pallas as pl
from jax.experimental.pallas import tpu as pltpu
from jax.sharding import PartitionSpec as P

MIB = 1024 * 1024
FULL = 62 * MIB
NT = (((1,), (1,)), ((), ()))


def cosine(phase, lon_count):
    turns = jnp.floor(phase * (1.0 / lon_count) + 0.5)
    folded = jnp.abs(phase - turns * lon_count)
    angle = (lon_count / 4 - folded) * (2.0 * math.pi / lon_count)
    square = angle * angle
    series = -1.0 / 39916800
    for factor in (1.0 / 362880, -1.0 / 5040, 1.0 / 120, -1.0 / 6, 1.0):
        series = series * square + factor
    return series * angle


def fourier_kernel(ids_ref, grid_hbm, out_ref, table, field, sem):
    step = pl.program_id(0)
    rows, lon_count = table.shape
    blocks = lon_count // 128
    middle = blocks // 2
    group = 16

    @pl.when(step == 0)
    def _():
        load = pltpu.make_async_copy(grid_hbm, field, sem)
        load.start()
        row = lax.broadcasted_iota(jnp.int32, (group, 128), 0)
        lane = lax.broadcasted_iota(jnp.int32, (group, 128), 1).astype(jnp.float32)
        offset = jnp.where((row & 1) == 1, lon_count // 4, 0).astype(jnp.float32)

        def fill(g, carry):
            start = pl.multiple_of(g * group, group)
            order = jnp.broadcast_to(ids_ref[pl.ds(start, group), :], (group, 128))
            scale = jnp.where(order == 0.0, 1.0, 2.0)
            double = 2.0 * cosine(order * 128.0, lon_count)
            below = scale * cosine(order * (lane + (middle - 1) * 128.0) + offset, lon_count)
            above = scale * cosine(order * (lane + middle * 128.0) + offset, lon_count)
            for a, first, second in ((middle - 1, above, below), (middle, below, above)):
                ahead = 1 if a == middle else -1
                while 0 <= a < blocks:
                    table[pl.ds(start, group), a * 128:(a + 1) * 128] = second.astype(jnp.bfloat16)
                    first, second = second, double * second - first
                    a += ahead
            return carry

        lax.fori_loop(0, rows // group, fill, 0, unroll=4)
        load.wait()

    share = rows // pl.num_programs(0)
    mine = pl.ds(pl.multiple_of(step * share, 16), share)
    spectra = lax.dot_general(table[mine, :], field[...], NT, preferred_element_type=jnp.float32)
    out_ref[...] = spectra.reshape(out_ref.shape).astype(jnp.bfloat16)


def fourier(grid_rows, order_ids, dests):
    points, lon_count = grid_rows.shape
    rows = 2 * order_ids.shape[0]
    steps = 4
    per_dest = rows // dests
    ids = jnp.repeat(order_ids, 2)[:, None].astype(jnp.float32)
    return pl.pallas_call(
        fourier_kernel,
        grid=(steps,),
        in_specs=[
            pl.BlockSpec((rows, 1), lambda s: (0, 0)),
            pl.BlockSpec(memory_space=pl.ANY),
        ],
        out_specs=pl.BlockSpec((dests // steps, per_dest, points), lambda s: (s, 0, 0)),
        out_shape=jax.ShapeDtypeStruct((dests, per_dest, points), jnp.bfloat16),
        scratch_shapes=[
            pltpu.VMEM((rows, lon_count), jnp.bfloat16),
            pltpu.VMEM((points, lon_count), jnp.bfloat16),
            pltpu.SemaphoreType.DMA,
        ],
        compiler_params=pltpu.CompilerParams(vmem_limit_bytes=FULL),
        name="fourier_analysis",
    )(ids, grid_rows)


def arrange_kernel(ids_ref, map_ref, leg_ref, out_ref, pick):
    j, step = pl.program_id(0), pl.program_id(1)
    span, cycles = leg_ref.shape[1:]

    @pl.when((j == 0) & (step == 0))
    def _():
        for r in range(0, cycles, 128):
            cycle = r + lax.broadcasted_iota(jnp.int32, (128, cycles), 0)
            pick[r:r + 128, :] = jnp.where(cycle == map_ref[...], 1.0, 0.0).astype(jnp.bfloat16)

    @pl.when((step + 1) * span > ids_ref[j])
    def _():
        out_ref[0] = jnp.dot(leg_ref[0], pick[...], preferred_element_type=jnp.float32).astype(jnp.bfloat16)


def arrange_legendre(own_orders, cycle_map, legendre, span):
    orders, degrees, cycles = legendre.shape
    return pl.pallas_call(
        arrange_kernel,
        grid_spec=pltpu.PrefetchScalarGridSpec(
            num_scalar_prefetch=1,
            grid=(orders, degrees // span),
            in_specs=[
                pl.BlockSpec((1, cycles), lambda j, s, ids: (0, 0)),
                pl.BlockSpec((1, span, cycles), lambda j, s, ids: (j, s, 0)),
            ],
            out_specs=pl.BlockSpec((1, span, cycles), lambda j, s, ids: (j, s, 0)),
            scratch_shapes=[pltpu.VMEM((cycles, cycles), jnp.bfloat16)],
        ),
        out_shape=jax.ShapeDtypeStruct(legendre.shape, jnp.bfloat16),
        compiler_params=pltpu.CompilerParams(vmem_limit_bytes=FULL),
        cost_estimate=pl.CostEstimate(
            flops=2 * orders * degrees * cycles * cycles, bytes_accessed=4 * orders * degrees * cycles, transcendentals=0),
        name="arrange_legendre",
    )(own_orders, cycle_map[None, :], legendre)


def legendre_kernel(ids_ref, got_hbm, leg_hbm, out_ref, got, leg, rows_z, spectra, rest, got_sems, leg_sems, *, ord_count, lev_count, lev_dev, cycles_dev, deg_block):
    step = pl.program_id(0)
    orders = leg.shape[0]
    pairs = 2 * orders
    levels = lev_count * lev_dev
    span = leg.shape[1] // pl.num_programs(0)

    def load_got(b):
        return pltpu.make_async_copy(got_hbm.at[:, b], got.at[:, b], got_sems.at[b])

    def load_leg(p):
        part = pl.ds(pl.multiple_of(p * span, 16), span)
        return pltpu.make_async_copy(leg_hbm.at[:, part, :], leg.at[:, part, :], leg_sems.at[p])

    @pl.when(step == 0)
    def _():
        for b in range(lev_count):
            load_got(b).start()
        for p in range(leg_sems.shape[0]):
            load_leg(p).start()

        def gather(b, carry):
            load_got(b).wait()
            for l in range(lev_dev):
                row = jnp.concatenate([
                    got[a, b, :, l * cycles_dev:(l + 1) * cycles_dev].astype(jnp.float32)
                    for a in range(ord_count)
                ], axis=1)
                for t in range(rows_z.shape[0]):
                    rows_z[t, pl.ds(b * lev_dev + l, pairs, stride=levels), :] = row[:, t * 128:(t + 1) * 128]
            return carry

        lax.fori_loop(0, lev_count, gather, 0)
        for j in range(orders):
            for t in range(rows_z.shape[0]):
                lanes = slice(t * 128, (t + 1) * 128)
                tails = []
                for c in range(2):
                    base = (2 * j + c) * levels
                    spectra[j, c * 128:(c + 1) * 128, lanes] = rows_z[t, base:base + 128, :].astype(jnp.bfloat16)
                    tails.append(rows_z[t, base + 128:base + levels, :])
                spectra[j, 256:, lanes] = jnp.concatenate(tails, axis=0).astype(jnp.bfloat16)

    load_leg(step).wait()
    here = pl.ds(pl.multiple_of(step * span, 16), span)
    for j in range(orders):
        order = ids_ref[j]
        degree = step * span + lax.broadcasted_iota(jnp.int32, (span, 1), 0)
        used = (step + 1) * span > order

        @pl.when(used)
        def _():
            product = lax.dot_general(leg[j, here, :], spectra[j], NT, preferred_element_type=jnp.float32)
            product = jnp.where(degree >= order, product, 0.0)
            for d in range(span // deg_block):
                own = product[d * deg_block:(d + 1) * deg_block]
                for c in range(2):
                    at = (2 * j + c) * deg_block
                    out_ref[d, at:at + deg_block, :] = own[:, c * 128:(c + 1) * 128].astype(jnp.bfloat16)
            rest[j, :, 0:16] = product[:, 256:]

        @pl.when(jnp.logical_not(used))
        def _():
            for d in range(span // deg_block):
                at = 2 * j * deg_block
                out_ref[d, at:at + 2 * deg_block, :] = jnp.zeros((2 * deg_block, 128), jnp.bfloat16)
            rest[j, :, 0:16] = jnp.zeros((span, 16), jnp.float32)

    tail = jnp.concatenate([rest[j, :, 0:16] for j in range(orders)], axis=1)
    half = deg_block // 2
    for d in range(span // deg_block):
        first = tail[d * deg_block:d * deg_block + half]
        second = tail[d * deg_block + half:(d + 1) * deg_block]
        out_ref[d, pairs * deg_block:, :] = jnp.concatenate([first, second], axis=1).astype(jnp.bfloat16)


def legendre_sums(own_orders, arrived, legendre, span, ord_count, lev_count, lev_dev, cycles_dev):
    orders, degrees, cycles = legendre.shape
    deg_block = degrees // lev_count
    per_step = span // deg_block
    steps = degrees // span
    packed = (2 * orders) * deg_block + deg_block // 2
    rows = 2 * orders * lev_count * lev_dev
    kernel = functools.partial(
        legendre_kernel, ord_count=ord_count, lev_count=lev_count, lev_dev=lev_dev,
        cycles_dev=cycles_dev, deg_block=deg_block)
    return pl.pallas_call(
        kernel,
        grid_spec=pltpu.PrefetchScalarGridSpec(
            num_scalar_prefetch=1,
            grid=(steps,),
            in_specs=[pl.BlockSpec(memory_space=pl.ANY)] * 2,
            out_specs=pl.BlockSpec((per_step, packed, 128), lambda s, ids: (s, 0, 0)),
            scratch_shapes=[
                pltpu.VMEM((ord_count, lev_count) + arrived.shape[1:], jnp.bfloat16),
                pltpu.VMEM(legendre.shape, jnp.bfloat16),
                pltpu.VMEM((cycles // 128, rows, 128), jnp.float32),
                pltpu.VMEM((orders, 2 * lev_count * lev_dev, cycles), jnp.bfloat16),
                pltpu.VMEM((orders, span, 128), jnp.float32),
                pltpu.SemaphoreType.DMA((lev_count,)),
                pltpu.SemaphoreType.DMA((steps,)),
            ],
        ),
        out_shape=jax.ShapeDtypeStruct((lev_count, packed, 128), jnp.bfloat16),
        compiler_params=pltpu.CompilerParams(vmem_limit_bytes=FULL),
        name="legendre_sums",
    )(own_orders, arrived.reshape((ord_count, lev_count) + arrived.shape[1:]), legendre)


def degrees_first_kernel(cov_ref, out_ref, front, back):
    step = pl.program_id(0)
    group, levels, deg_block = cov_ref.shape
    last = pl.num_programs(0) - 1

    @pl.when(step < last)
    def _():
        for g in range(group):
            block = cov_ref[g].astype(jnp.float32)
            at = pl.ds(step * group + g, deg_block, stride=levels)
            front[at, :] = block[:128].T
            back[at, :] = jnp.concatenate([block[128:], jnp.zeros((120, deg_block), jnp.float32)], axis=0).T

    @pl.when(step == last)
    def _():
        def narrow(n, carry):
            rows = pl.ds(pl.multiple_of(n * levels, 8), levels)
            out_ref[n, :, 0:128] = front[rows, :].astype(jnp.bfloat16)
            out_ref[n, :, 128:] = back[rows, :].astype(jnp.bfloat16)
            return carry

        lax.fori_loop(0, deg_block, narrow, 0, unroll=4)


def degrees_first(cov_levels):
    levels, _, deg_block = cov_levels.shape
    group = 17
    steps = levels // group
    return pl.pallas_call(
        degrees_first_kernel,
        grid=(steps + 1,),
        in_specs=[pl.BlockSpec((group, levels, deg_block), lambda s: (jnp.minimum(s, steps - 1), 0, 0))],
        out_specs=pl.BlockSpec((deg_block, levels, 256), lambda s: (0, 0, 0), pipeline_mode=pl.Buffered(1)),
        out_shape=jax.ShapeDtypeStruct((deg_block, levels, 256), jnp.bfloat16),
        scratch_shapes=[pltpu.VMEM((deg_block * levels, 128), jnp.float32)] * 2,
        compiler_params=pltpu.CompilerParams(vmem_limit_bytes=FULL),
        cost_estimate=pl.CostEstimate(flops=10**9, bytes_accessed=3 * 10**7, transcendentals=0),
        name="degrees_first",
    )(cov_levels)


def covariance_kernel(got_ref, cov_hbm, out_ref, cov, main, rest, out_main, out_rest, sems, *, pairs):
    step = pl.program_id(0)
    sources = got_ref.shape[0]
    deg_block, levels, _ = cov.shape
    half = deg_block // 2
    rows = sources * pairs
    pitch = main.shape[0] // rows
    pieces = sems.shape[0]
    piece = deg_block // pieces

    def load(p):
        part = pl.ds(p * piece, piece)
        return pltpu.make_async_copy(cov_hbm.at[part], cov.at[part], sems.at[p])

    @pl.when(step == 0)
    def _():
        for p in range(pieces):
            load(p).start()

        def unpack(s, carry):
            tail = got_ref[s, pairs * deg_block:, :].astype(jnp.float32)
            for r in range(pairs):
                base = pl.multiple_of((s * pairs + r) * pitch, 8)
                main[pl.ds(base, deg_block), :] = got_ref[s, r * deg_block:(r + 1) * deg_block, :].astype(jnp.float32)
                for h in range(2):
                    at = h * 64 + r * 8
                    moved = tail if at == 0 else pltpu.roll(tail, 128 - at, 1)
                    rest[pl.ds(base + h * half, half), :] = moved
            return carry

        lax.fori_loop(0, sources, unpack, 0)

        def multiply(n, carry):
            left = jnp.concatenate([
                main[pl.ds(n, rows, stride=pitch), :],
                rest[pl.ds(n, rows, stride=pitch), :]], axis=1)[:, :levels].astype(jnp.bfloat16)
            product = jnp.dot(left, cov[n], preferred_element_type=jnp.float32)
            out_main[pl.ds(n, rows, stride=pitch), :] = product[:, :128]
            out_rest[pl.ds(n, rows, stride=pitch), :] = product[:, 128:]
            return carry

        def share(p, carry):
            load(p).wait()
            for i in range(piece):
                multiply(p * piece + i, carry)
            return carry

        lax.fori_loop(0, pieces, share, 0)

    for r in range(pairs):
        base = pl.multiple_of((step * pairs + r) * pitch, 8)
        out_ref[r // 2, r % 2, 0:128, :] = out_main[pl.ds(base, deg_block), :].T
        out_ref[r // 2, r % 2, 128:, :] = out_rest[pl.ds(base, deg_block), :][:, :levels - 128].T


def covariance(arrived, cov, orders):
    sources = arrived.shape[0]
    deg_block, levels, wide = cov.shape
    order_block = orders // sources
    rows = 2 * orders * (deg_block + 8)
    return pl.pallas_call(
        functools.partial(covariance_kernel, pairs=2 * order_block),
        grid=(sources,),
        in_specs=[
            pl.BlockSpec(memory_space=pltpu.VMEM),
            pl.BlockSpec(memory_space=pl.ANY),
        ],
        out_specs=pl.BlockSpec((order_block, 2, levels, deg_block), lambda s: (s, 0, 0, 0)),
        out_shape=jax.ShapeDtypeStruct((orders, 2, levels, deg_block), jnp.float32),
        scratch_shapes=[pltpu.VMEM(cov.shape, jnp.bfloat16)] + [pltpu.VMEM((rows, 128), jnp.float32)] * 4 + [
            pltpu.SemaphoreType.DMA((10,))],
        compiler_params=pltpu.CompilerParams(vmem_limit_bytes=56 * MIB),
        name="vertical_covariance",
    )(arrived, cov)


def shards(grid_grad, legendre, cov_root, order_ids, cycle_map):
    cycles_dev, lev_dev, lon_count = grid_grad.shape
    orders_dev, degree_count, cycle_total = legendre.shape
    ord_count = lax.axis_size("ord")
    lev_count = lax.axis_size("lev")
    dests = ord_count * lev_count
    grid_rows = grid_grad.transpose(1, 0, 2).reshape(lev_dev * cycles_dev, lon_count)
    spectra = fourier(grid_rows, order_ids, dests)
    position = lax.axis_index("ord") * lev_count + lax.axis_index("lev")
    own_orders = lax.dynamic_slice_in_dim(order_ids, position * orders_dev, orders_dev, 0)
    span = 2 * degree_count // lev_count
    spectra, cycle_map = lax.optimization_barrier((spectra, cycle_map))
    arranged = arrange_legendre(own_orders, cycle_map, legendre, span)
    arrived = lax.all_to_all(spectra, ("ord", "lev"), split_axis=0, concat_axis=0, tiled=True)
    packed = legendre_sums(own_orders, arrived, arranged, span, ord_count, lev_count, lev_dev, cycles_dev)
    swapped = lax.all_to_all(packed, "lev", split_axis=0, concat_axis=0, tiled=True)
    cov = degrees_first(cov_root.transpose(1, 2, 0))
    out = covariance(swapped, cov, orders_dev * lev_count)
    return out.transpose(3, 0, 1, 2)


def solution(mesh):
    return jax.shard_map(
        shards,
        mesh=mesh,
        in_specs=(
            P("ord", "lev", None),
            P(("ord", "lev"), None, None),
            P("lev", None, None),
            P(),
            P(),
        ),
        out_specs=P("lev", "ord", None, None),
        check_vma=False,
    )
```

```python
import functools
import math

import jax
import jax.numpy as jnp
from jax import lax
from jax.experimental import pallas as pl
from jax.experimental.pallas import tpu as pltpu
from jax.sharding import PartitionSpec as P

MIB = 1024 * 1024
FULL = 62 * MIB
NT = (((1,), (1,)), ((), ()))


def cosine(phase, lon_count):
    turns = jnp.floor(phase * (1.0 / lon_count) + 0.5)
    folded = jnp.abs(phase - turns * lon_count)
    angle = (lon_count / 4 - folded) * (2.0 * math.pi / lon_count)
    square = angle * angle
    series = -1.0 / 39916800
    for factor in (1.0 / 362880, -1.0 / 5040, 1.0 / 120, -1.0 / 6, 1.0):
        series = series * square + factor
    return series * angle


def fourier_kernel(ids_ref, grid_hbm, out_ref, table, field, sem, *, orders_dev, per, half):
    step = pl.program_id(0)
    rows, lon_count = table.shape
    blocks = lon_count // 128
    middle = blocks // 2
    group = 16

    @pl.when(step == 0)
    def _():
        load = pltpu.make_async_copy(grid_hbm, field, sem)
        load.start()
        row = lax.broadcasted_iota(jnp.int32, (group, 128), 0)
        lane = lax.broadcasted_iota(jnp.int32, (group, 128), 1).astype(jnp.float32)
        offset = jnp.where((row & 1) == 1, lon_count // 4, 0).astype(jnp.float32)

        def fill(g, carry):
            start = pl.multiple_of(g * group, group)
            order = jnp.zeros((group, 128), jnp.int32)
            for i in range(group // 2):
                k = g * (group // 2) + i
                order = jnp.where(row // 2 == i, ids_ref[k // per * orders_dev + half * per + k % per], order)
            order = order.astype(jnp.float32)
            scale = jnp.where(order == 0.0, 1.0, 2.0)
            double = 2.0 * cosine(order * 128.0, lon_count)
            below = scale * cosine(order * (lane + (middle - 1) * 128.0) + offset, lon_count)
            above = scale * cosine(order * (lane + middle * 128.0) + offset, lon_count)
            for a, first, second in ((middle - 1, above, below), (middle, below, above)):
                ahead = 1 if a == middle else -1
                while 0 <= a < blocks:
                    table[pl.ds(start, group), a * 128:(a + 1) * 128] = second.astype(jnp.bfloat16)
                    first, second = second, double * second - first
                    a += ahead
            return carry

        lax.fori_loop(0, rows // group, fill, 0, unroll=4)
        load.wait()

    share = rows // pl.num_programs(0)
    mine = pl.ds(pl.multiple_of(step * share, 16), share)
    spectra = lax.dot_general(table[mine, :], field[...], NT, preferred_element_type=jnp.float32)
    out_ref[...] = spectra.reshape(out_ref.shape).astype(jnp.bfloat16)


def fourier(grid_rows, order_ids, dests, per, half):
    points, lon_count = grid_rows.shape
    orders_dev = order_ids.shape[0] // dests
    rows = 2 * dests * per
    steps = per
    kernel = functools.partial(fourier_kernel, orders_dev=orders_dev, per=per, half=half)
    return pl.pallas_call(
        kernel,
        grid_spec=pltpu.PrefetchScalarGridSpec(
            num_scalar_prefetch=1,
            grid=(steps,),
            in_specs=[pl.BlockSpec(memory_space=pl.ANY)],
            out_specs=pl.BlockSpec((dests // steps, 2 * per, points), lambda s, ids: (s, 0, 0)),
            scratch_shapes=[
                pltpu.VMEM((rows, lon_count), jnp.bfloat16),
                pltpu.VMEM((points, lon_count), jnp.bfloat16),
                pltpu.SemaphoreType.DMA,
            ],
        ),
        out_shape=jax.ShapeDtypeStruct((dests, 2 * per, points), jnp.bfloat16),
        compiler_params=pltpu.CompilerParams(vmem_limit_bytes=FULL),
        cost_estimate=pl.CostEstimate(flops=2 * rows * points * lon_count, bytes_accessed=10 * MIB, transcendentals=0),
        name="fourier_analysis",
    )(order_ids, grid_rows)


def arrange_kernel(ids_ref, map_ref, leg_ref, out_ref, pick):
    j, step = pl.program_id(0), pl.program_id(1)
    span, cycles = leg_ref.shape[1:]

    @pl.when((j == 0) & (step == 0))
    def _():
        for r in range(0, cycles, 128):
            cycle = r + lax.broadcasted_iota(jnp.int32, (128, cycles), 0)
            pick[r:r + 128, :] = jnp.where(cycle == map_ref[...], 1.0, 0.0).astype(jnp.bfloat16)

    @pl.when((step + 1) * span > ids_ref[j])
    def _():
        out_ref[0] = jnp.dot(leg_ref[0], pick[...], preferred_element_type=jnp.float32).astype(jnp.bfloat16)


def arrange_legendre(own_orders, cycle_map, legendre, span):
    orders, degrees, cycles = legendre.shape
    return pl.pallas_call(
        arrange_kernel,
        grid_spec=pltpu.PrefetchScalarGridSpec(
            num_scalar_prefetch=1,
            grid=(orders, degrees // span),
            in_specs=[
                pl.BlockSpec((1, cycles), lambda j, s, ids: (0, 0)),
                pl.BlockSpec((1, span, cycles), lambda j, s, ids: (j, jnp.maximum(s, ids[j] // span), 0)),
            ],
            out_specs=pl.BlockSpec((1, span, cycles), lambda j, s, ids: (j, jnp.maximum(s, ids[j] // span), 0)),
            scratch_shapes=[pltpu.VMEM((cycles, cycles), jnp.bfloat16)],
        ),
        out_shape=jax.ShapeDtypeStruct(legendre.shape, jnp.bfloat16),
        compiler_params=pltpu.CompilerParams(vmem_limit_bytes=FULL),
        cost_estimate=pl.CostEstimate(
            flops=2 * orders * degrees * cycles * cycles, bytes_accessed=4 * orders * degrees * cycles, transcendentals=0),
        name="arrange_legendre",
    )(own_orders, cycle_map[None, :], legendre)


def tail_rows(deg_block, per):
    return -(-deg_block * 16 * per // 128 // 16) * 16


def legendre_kernel(ids_ref, dests_ref, got_hbm, leg_hbm, *refs, lev_dev, cycles_dev, deg_block, half):
    count = dests_ref.shape[0]
    outs = refs[:count]
    got, leg, rows_z, spectra, rest, send, got_sems, leg_sems, out_sems = refs[count:]
    ord_count, lev_count = got.shape[:2]
    per = leg.shape[0]
    pairs = 2 * per
    levels = lev_count * lev_dev
    span = 2 * deg_block
    steps = count // 2

    def load_got(b):
        return pltpu.make_async_copy(got_hbm.at[:, b], got.at[:, b], got_sems.at[b])

    def load_leg(k):
        source = leg_hbm.at[pl.ds(half * per, per), pl.ds(pl.multiple_of(dests_ref[k] * deg_block, 16), deg_block), :]
        return pltpu.make_async_copy(source, leg.at[:, pl.ds(k * deg_block, deg_block), :], leg_sems.at[k])

    for b in range(lev_count):
        load_got(b).start()
    def gather(b, carry):
        load_got(b).wait()
        load_leg(b).start()
        for l in range(lev_dev):
            row = jnp.concatenate([
                got[a, b, :, l * cycles_dev:(l + 1) * cycles_dev].astype(jnp.float32) for a in range(ord_count)
            ], axis=1)
            for t in range(rows_z.shape[0]):
                rows_z[t, pl.ds(b * lev_dev + l, pairs, stride=levels), :] = row[:, t * 128:(t + 1) * 128]
        return carry

    lax.fori_loop(0, lev_count, gather, 0)
    for j in range(per):
        for t in range(rows_z.shape[0]):
            lanes = slice(t * 128, (t + 1) * 128)
            tails = []
            for c in range(2):
                base = (2 * j + c) * levels
                spectra[j, c * 128:(c + 1) * 128, lanes] = rows_z[t, base:base + 128, :].astype(jnp.bfloat16)
                tails.append(rows_z[t, base + 128:base + levels, :])
            spectra[j, 256:, lanes] = jnp.concatenate(tails, axis=0).astype(jnp.bfloat16)

    row = lax.broadcasted_iota(jnp.int32, (span, 1), 0)
    groups = 128 // (16 * per)
    chunk = deg_block // groups
    for step in range(steps):
        load_leg(2 * step).wait()
        load_leg(2 * step + 1).wait()
        first, second = dests_ref[2 * step], dests_ref[2 * step + 1]
        degree = jnp.where(row < deg_block, first * deg_block + row, (second - 1) * deg_block + row)
        for j in range(per):
            order = ids_ref[half * per + j]
            used = (first // 2 + 1) * span > order

            @pl.when(used)
            def _():
                here = slice(step * span, (step + 1) * span)
                product = lax.dot_general(leg[j, here, :], spectra[j], NT, preferred_element_type=jnp.float32)
                product = jnp.where(degree >= order, product, 0.0)
                for d in range(2):
                    own = product[d * deg_block:(d + 1) * deg_block]
                    for c in range(2):
                        at = (2 * j + c) * deg_block
                        send[2 * step + d, at:at + deg_block, :] = own[:, c * 128:(c + 1) * 128].astype(jnp.bfloat16)
                rest[j, :, 0:16] = product[:, 256:]

            @pl.when(jnp.logical_not(used))
            def _():
                for d in range(2):
                    at = 2 * j * deg_block
                    send[2 * step + d, at:at + 2 * deg_block, :] = jnp.zeros((2 * deg_block, 128), jnp.bfloat16)
                rest[j, :, 0:16] = jnp.zeros((span, 16), jnp.float32)

        tail = jnp.concatenate([rest[j, :, 0:16] for j in range(per)], axis=1)
        for d in range(2):
            packed = jnp.concatenate([
                tail[d * deg_block + g * chunk:d * deg_block + (g + 1) * chunk] for g in range(groups)], axis=1)
            at = pairs * deg_block
            send[2 * step + d, at:at + chunk, :] = packed.astype(jnp.bfloat16)
            k = 2 * step + d
            pltpu.make_async_copy(send.at[k], outs[k], out_sems.at[k]).start()
    for k in range(count):
        pltpu.make_async_copy(send.at[k], outs[k], out_sems.at[k]).wait()


def legendre_sums(own_orders, dests, arrived, legendre, per, half, lev_dev, cycles_dev):
    _, degrees, cycles = legendre.shape
    ord_count, lev_count = arrived.shape[:2]
    deg_block = degrees // lev_count
    packed = 2 * per * deg_block + tail_rows(deg_block, per)
    kernel = functools.partial(legendre_kernel, lev_dev=lev_dev, cycles_dev=cycles_dev, deg_block=deg_block, half=half)
    anywhere = pl.BlockSpec(memory_space=pl.ANY)
    return pl.pallas_call(
        kernel,
        grid_spec=pltpu.PrefetchScalarGridSpec(
            num_scalar_prefetch=2,
            grid=(),
            in_specs=[anywhere] * 2,
            out_specs=[anywhere] * lev_count,
            scratch_shapes=[
                pltpu.VMEM(arrived.shape, jnp.bfloat16),
                pltpu.VMEM((per, degrees, cycles), jnp.bfloat16),
                pltpu.VMEM((cycles // 128, 2 * per * lev_count * lev_dev, 128), jnp.float32),
                pltpu.VMEM((per, 2 * lev_count * lev_dev, cycles), jnp.bfloat16),
                pltpu.VMEM((per, 2 * deg_block, 128), jnp.float32),
                pltpu.VMEM((lev_count, packed, 128), jnp.bfloat16),
                pltpu.SemaphoreType.DMA((lev_count,)),
                pltpu.SemaphoreType.DMA((lev_count,)),
                pltpu.SemaphoreType.DMA((lev_count,)),
            ],
        ),
        out_shape=[jax.ShapeDtypeStruct((packed, 128), jnp.bfloat16)] * lev_count,
        compiler_params=pltpu.CompilerParams(vmem_limit_bytes=FULL),
        cost_estimate=pl.CostEstimate(flops=3 * 10**9, bytes_accessed=20 * MIB, transcendentals=0),
        name="legendre_sums",
    )(own_orders, dests, arrived, legendre)


def degrees_first_kernel(cov_ref, out_ref, front, back):
    step = pl.program_id(0)
    group, levels, deg_block = cov_ref.shape
    last = pl.num_programs(0) - 1

    @pl.when(step < last)
    def _():
        for g in range(group):
            block = cov_ref[g].astype(jnp.float32)
            at = pl.ds(step * group + g, deg_block, stride=levels)
            front[at, :] = block[:128].T
            back[at, :] = jnp.concatenate([block[128:], jnp.zeros((120, deg_block), jnp.float32)], axis=0).T

    @pl.when(step == last)
    def _():
        def narrow(n, carry):
            rows = pl.ds(pl.multiple_of(n * levels, 8), levels)
            out_ref[n, :, 0:128] = front[rows, :].astype(jnp.bfloat16)
            out_ref[n, :, 128:] = back[rows, :].astype(jnp.bfloat16)
            return carry

        lax.fori_loop(0, deg_block, narrow, 0, unroll=4)


def degrees_first(cov_levels):
    levels, _, deg_block = cov_levels.shape
    group = 17
    steps = levels // group
    return pl.pallas_call(
        degrees_first_kernel,
        grid=(steps + 1,),
        in_specs=[pl.BlockSpec((group, levels, deg_block), lambda s: (jnp.minimum(s, steps - 1), 0, 0))],
        out_specs=pl.BlockSpec((deg_block, levels, 256), lambda s: (0, 0, 0), pipeline_mode=pl.Buffered(1)),
        out_shape=jax.ShapeDtypeStruct((deg_block, levels, 256), jnp.bfloat16),
        scratch_shapes=[pltpu.VMEM((deg_block * levels, 128), jnp.float32)] * 2,
        compiler_params=pltpu.CompilerParams(vmem_limit_bytes=FULL),
        cost_estimate=pl.CostEstimate(flops=10**9, bytes_accessed=3 * 10**7, transcendentals=0),
        name="degrees_first",
    )(cov_levels)


def covariance_kernel(place_ref, *refs, per, count, carried):
    got_hbm, cov_hbm = refs[:count], refs[count]
    out_ref, gots, cov, main, rest, out_main, out_rest, got_sems, cov_sems = refs[count + 1 + carried:]
    step = pl.program_id(0)
    deg_block, levels, _ = cov.shape
    pairs = 2 * per
    groups = 128 // (8 * pairs)
    chunk = deg_block // groups
    rows = count * pairs
    pitch = main.shape[0] // rows
    pieces = cov_sems.shape[0]
    piece = deg_block // pieces

    def load_got(s):
        return pltpu.make_async_copy(got_hbm[s], gots.at[s], got_sems.at[s])

    def load_cov(p):
        part = pl.ds(p * piece, piece)
        return pltpu.make_async_copy(cov_hbm.at[part], cov.at[part], cov_sems.at[p])

    @pl.when(step == 0)
    def _():
        for s in range(count):
            load_got(s).start()
        for p in range(2):
            load_cov(p).start()
        for s in range(count):
            load_got(s).wait()
            at = pairs * deg_block
            tail = gots[s, at:at + chunk, :].astype(jnp.float32)
            for r in range(pairs):
                base = (s * pairs + r) * pitch
                main[base:base + deg_block, :] = gots[s, r * deg_block:(r + 1) * deg_block, :].astype(jnp.float32)
                for g in range(groups):
                    lane = (g * pairs + r) * 8
                    moved = tail if lane == 0 else pltpu.roll(tail, 128 - lane, 1)
                    rest[base + g * chunk:base + (g + 1) * chunk, :] = moved

        def multiply(n, carry):
            left = jnp.concatenate([
                main[pl.ds(n, rows, stride=pitch), :],
                rest[pl.ds(n, rows, stride=pitch), :]], axis=1)[:, :levels].astype(jnp.bfloat16)
            product = jnp.dot(left, cov[n], preferred_element_type=jnp.float32)
            out_main[pl.ds(n, rows, stride=pitch), :] = product[:, :128]
            out_rest[pl.ds(n, rows, stride=pitch), :] = product[:, 128:]
            return carry

        def share(p, carry):
            load_cov(p).wait()

            @pl.when(p + 2 < pieces)
            def _():
                load_cov(p + 2).start()

            for i in range(piece):
                multiply(p * piece + i, carry)
            return carry

        lax.fori_loop(0, pieces, share, 0)

    for r in range(pairs):
        base = pl.multiple_of((step * pairs + r) * pitch, 8)
        out_ref[r // 2, r % 2, 0:128, :] = out_main[pl.ds(base, deg_block), :].T
        out_ref[r // 2, r % 2, 128:, :] = out_rest[pl.ds(base, deg_block), :][:, :levels - 128].T


def covariance(places, arrived, cov, out, orders, per, half, halves):
    count = len(arrived)
    deg_block, levels, wide = cov.shape
    rows = count * 2 * per * (deg_block + 8)
    carried = 0 if out is None else 1
    anywhere = pl.BlockSpec(memory_space=pl.ANY)
    return pl.pallas_call(
        functools.partial(covariance_kernel, per=per, count=count, carried=carried),
        grid_spec=pltpu.PrefetchScalarGridSpec(
            num_scalar_prefetch=1,
            grid=(count,),
            in_specs=[anywhere] * (count + 1 + carried),
            out_specs=pl.BlockSpec((per, 2, levels, deg_block), lambda s, place: (place[s] * halves + half, 0, 0, 0)),
            scratch_shapes=[
                pltpu.VMEM((count,) + arrived[0].shape, jnp.bfloat16),
                pltpu.VMEM(cov.shape, jnp.bfloat16),
            ] + [pltpu.VMEM((rows, 128), jnp.float32)] * 4 + [
                pltpu.SemaphoreType.DMA((count,)),
                pltpu.SemaphoreType.DMA((10,)),
            ],
        ),
        out_shape=jax.ShapeDtypeStruct((orders, 2, levels, deg_block), jnp.float32),
        input_output_aliases={count + 2: 0} if carried else {},
        compiler_params=pltpu.CompilerParams(vmem_limit_bytes=FULL),
        cost_estimate=pl.CostEstimate(flops=2 * 10**9, bytes_accessed=16 * MIB, transcendentals=0),
        name="vertical_covariance",
    )(places, *arrived, cov, *([out] if carried else []))


HALVES = 1


def shards(grid_grad, legendre, cov_root, order_ids, cycle_map):
    cycles_dev, lev_dev, lon_count = grid_grad.shape
    orders_dev, degree_count, cycle_total = legendre.shape
    ord_count = lax.axis_size("ord")
    lev_count = lax.axis_size("lev")
    dests = ord_count * lev_count
    chips = lev_count // 2
    per = orders_dev // HALVES
    lev = lax.axis_index("lev")
    position = lax.axis_index("ord") * lev_count + lev
    own_orders = lax.dynamic_slice_in_dim(order_ids, position * orders_dev, orders_dev, 0)
    grid_rows = grid_grad.transpose(1, 0, 2).reshape(lev_dev * cycles_dev, lon_count)

    near = [(d, f) for d in (1, chips - 1) for f in (0, 1)]
    far = [(d, f) for d in range(2, chips - 1) for f in (0, 1)]
    home = [(0, 1), (0, 0)]
    moves = near + far + home

    def moved(rank, d, f):
        return (rank // 2 + d) % chips * 2 + (rank % 2 + f) % 2

    targets = jnp.stack([moved(lev, d, f) for d, f in moves]).astype(jnp.int32)

    spectra = [fourier(grid_rows, order_ids, dests, per, 0)]
    spectra[0], cycle_map, cov_root = lax.optimization_barrier((spectra[0], cycle_map, cov_root))
    arranged = arrange_legendre(own_orders, cycle_map, legendre, 2 * degree_count // lev_count)
    cov = degrees_first(cov_root.transpose(1, 2, 0))
    arranged, cov = lax.optimization_barrier((arranged, cov))
    arrived = []
    for h in range(HALVES):
        if h > 0:
            spectra.append(fourier(grid_rows, order_ids, dests, per, h))
        blocks = lax.all_to_all(spectra[h], ("ord", "lev"), split_axis=0, concat_axis=0, tiled=True)
        blocks = blocks.reshape((ord_count, lev_count) + blocks.shape[1:])
        packed = legendre_sums(own_orders, targets, blocks, arranged, per, h, lev_dev, cycles_dev)
        sent = dict(zip(moves, packed))
        got = {(0, 0): sent[0, 0]}

        def exchange(some):
            for d, f in some:
                pairs = [(rank, moved(rank, d, f)) for rank in range(lev_count)]
                got[d, f] = lax.ppermute(sent[d, f], "lev", pairs)

        exchange(near + home[:1])
        held = near + far
        tied = lax.optimization_barrier([got[m] for m in near] + [sent[m] for m in far])
        for m, block in zip(held, tied):
            (got if m in near else sent)[m] = block
        exchange(far)
        arrived.append(got)

    out = None
    for h in range(HALVES):
        for some in (home + near, far):
            places = jnp.stack([moved(lev, chips - d, f) for d, f in some]).astype(jnp.int32)
            out = covariance(places, [arrived[h][m] for m in some], cov, out, orders_dev * lev_count, per, h, HALVES)
    return out.transpose(3, 0, 1, 2)


def solution(mesh):
    return jax.shard_map(
        shards,
        mesh=mesh,
        in_specs=(
            P("ord", "lev", None),
            P(("ord", "lev"), None, None),
            P("lev", None, None),
            P(),
            P(),
        ),
        out_specs=P("lev", "ord", None, None),
        check_vma=False,
    )
```

```python
import functools
import math

import jax
import jax.numpy as jnp
from jax import lax
from jax.experimental import pallas as pl
from jax.experimental.pallas import tpu as pltpu
from jax.sharding import PartitionSpec as P

MIB = 1024 * 1024
FULL = 62 * MIB
NT = (((1,), (1,)), ((), ()))


def cosine(phase, lon_count):
    turns = jnp.floor(phase * (1.0 / lon_count) + 0.5)
    folded = jnp.abs(phase - turns * lon_count)
    angle = (lon_count / 4 - folded) * (2.0 * math.pi / lon_count)
    square = angle * angle
    series = -1.0 / 39916800
    for factor in (1.0 / 362880, -1.0 / 5040, 1.0 / 120, -1.0 / 6, 1.0):
        series = series * square + factor
    return series * angle


def fourier_kernel(ids_ref, grid_hbm, out_ref, table, field, sem, *, orders_dev, per, half):
    step = pl.program_id(0)
    rows, lon_count = table.shape
    blocks = lon_count // 128
    middle = blocks // 2
    group = 16

    @pl.when(step == 0)
    def _():
        load = pltpu.make_async_copy(grid_hbm, field, sem)
        load.start()
        row = lax.broadcasted_iota(jnp.int32, (group, 128), 0)
        lane = lax.broadcasted_iota(jnp.int32, (group, 128), 1).astype(jnp.float32)
        offset = jnp.where((row & 1) == 1, lon_count // 4, 0).astype(jnp.float32)

        def fill(g, carry):
            start = pl.multiple_of(g * group, group)
            order = jnp.zeros((group, 128), jnp.int32)
            for i in range(group // 2):
                k = g * (group // 2) + i
                order = jnp.where(row // 2 == i, ids_ref[k // per * orders_dev + half * per + k % per], order)
            order = order.astype(jnp.float32)
            scale = jnp.where(order == 0.0, 1.0, 2.0)
            double = 2.0 * cosine(order * 128.0, lon_count)
            below = scale * cosine(order * (lane + (middle - 1) * 128.0) + offset, lon_count)
            above = scale * cosine(order * (lane + middle * 128.0) + offset, lon_count)
            for a, first, second in ((middle - 1, above, below), (middle, below, above)):
                ahead = 1 if a == middle else -1
                while 0 <= a < blocks:
                    table[pl.ds(start, group), a * 128:(a + 1) * 128] = second.astype(jnp.bfloat16)
                    first, second = second, double * second - first
                    a += ahead
            return carry

        lax.fori_loop(0, rows // group, fill, 0, unroll=4)
        load.wait()

    share = rows // pl.num_programs(0)
    mine = pl.ds(pl.multiple_of(step * share, 16), share)
    spectra = lax.dot_general(table[mine, :], field[...], NT, preferred_element_type=jnp.float32)
    out_ref[...] = spectra.reshape(out_ref.shape).astype(jnp.bfloat16)


def fourier(grid_rows, order_ids, dests, per, half):
    points, lon_count = grid_rows.shape
    orders_dev = order_ids.shape[0] // dests
    rows = 2 * dests * per
    steps = per
    kernel = functools.partial(fourier_kernel, orders_dev=orders_dev, per=per, half=half)
    return pl.pallas_call(
        kernel,
        grid_spec=pltpu.PrefetchScalarGridSpec(
            num_scalar_prefetch=1,
            grid=(steps,),
            in_specs=[pl.BlockSpec(memory_space=pl.ANY)],
            out_specs=pl.BlockSpec((dests // steps, 2 * per, points), lambda s, ids: (s, 0, 0)),
            scratch_shapes=[
                pltpu.VMEM((rows, lon_count), jnp.bfloat16),
                pltpu.VMEM((points, lon_count), jnp.bfloat16),
                pltpu.SemaphoreType.DMA,
            ],
        ),
        out_shape=jax.ShapeDtypeStruct((dests, 2 * per, points), jnp.bfloat16),
        compiler_params=pltpu.CompilerParams(vmem_limit_bytes=FULL),
        cost_estimate=pl.CostEstimate(flops=2 * rows * points * lon_count, bytes_accessed=10 * MIB, transcendentals=0),
        name="fourier_analysis",
    )(order_ids, grid_rows)


def arrange_kernel(ids_ref, map_ref, leg_ref, out_ref, pick):
    j, step = pl.program_id(0), pl.program_id(1)
    span, cycles = leg_ref.shape[1:]

    @pl.when((j == 0) & (step == 0))
    def _():
        for r in range(0, cycles, 128):
            cycle = r + lax.broadcasted_iota(jnp.int32, (128, cycles), 0)
            pick[r:r + 128, :] = jnp.where(cycle == map_ref[...], 1.0, 0.0).astype(jnp.bfloat16)

    @pl.when((step + 1) * span > ids_ref[j])
    def _():
        out_ref[0] = jnp.dot(leg_ref[0], pick[...], preferred_element_type=jnp.float32).astype(jnp.bfloat16)


def arrange_legendre(own_orders, cycle_map, legendre, span):
    orders, degrees, cycles = legendre.shape
    return pl.pallas_call(
        arrange_kernel,
        grid_spec=pltpu.PrefetchScalarGridSpec(
            num_scalar_prefetch=1,
            grid=(orders, degrees // span),
            in_specs=[
                pl.BlockSpec((1, cycles), lambda j, s, ids: (0, 0)),
                pl.BlockSpec((1, span, cycles), lambda j, s, ids: (j, jnp.maximum(s, ids[j] // span), 0)),
            ],
            out_specs=pl.BlockSpec((1, span, cycles), lambda j, s, ids: (j, jnp.maximum(s, ids[j] // span), 0)),
            scratch_shapes=[pltpu.VMEM((cycles, cycles), jnp.bfloat16)],
        ),
        out_shape=jax.ShapeDtypeStruct(legendre.shape, jnp.bfloat16),
        compiler_params=pltpu.CompilerParams(vmem_limit_bytes=FULL),
        cost_estimate=pl.CostEstimate(
            flops=2 * orders * degrees * cycles * cycles, bytes_accessed=4 * orders * degrees * cycles, transcendentals=0),
        name="arrange_legendre",
    )(own_orders, cycle_map[None, :], legendre)


def tail_rows(deg_block, per):
    return -(-deg_block * 16 * per // 128 // 16) * 16


def legendre_kernel(ids_ref, dests_ref, got_hbm, leg_hbm, *refs, lev_dev, cycles_dev, deg_block, half):
    count = dests_ref.shape[0]
    outs = refs[:count]
    got, leg, rows_z, spectra, rest, send, got_sems, leg_sems, out_sems = refs[count:]
    ord_count, lev_count = got.shape[:2]
    per = leg.shape[0]
    pairs = 2 * per
    levels = lev_count * lev_dev
    span = 2 * deg_block
    steps = count // 2

    def load_got(b):
        return pltpu.make_async_copy(got_hbm.at[:, b], got.at[:, b], got_sems.at[b])

    def load_leg(k):
        source = leg_hbm.at[pl.ds(half * per, per), pl.ds(pl.multiple_of(dests_ref[k] * deg_block, 16), deg_block), :]
        return pltpu.make_async_copy(source, leg.at[:, pl.ds(k * deg_block, deg_block), :], leg_sems.at[k])

    for b in range(lev_count):
        load_got(b).start()
    def gather(b, carry):
        load_got(b).wait()
        load_leg(b).start()
        for l in range(lev_dev):
            row = jnp.concatenate([
                got[a, b, :, l * cycles_dev:(l + 1) * cycles_dev].astype(jnp.float32) for a in range(ord_count)
            ], axis=1)
            for t in range(rows_z.shape[0]):
                rows_z[t, pl.ds(b * lev_dev + l, pairs, stride=levels), :] = row[:, t * 128:(t + 1) * 128]
        return carry

    lax.fori_loop(0, lev_count, gather, 0)
    for j in range(per):
        for t in range(rows_z.shape[0]):
            lanes = slice(t * 128, (t + 1) * 128)
            tails = []
            for c in range(2):
                base = (2 * j + c) * levels
                spectra[j, c * 128:(c + 1) * 128, lanes] = rows_z[t, base:base + 128, :].astype(jnp.bfloat16)
                tails.append(rows_z[t, base + 128:base + levels, :])
            spectra[j, 256:, lanes] = jnp.concatenate(tails, axis=0).astype(jnp.bfloat16)

    row = lax.broadcasted_iota(jnp.int32, (span, 1), 0)
    groups = 128 // (16 * per)
    chunk = deg_block // groups
    for step in range(steps):
        load_leg(2 * step).wait()
        load_leg(2 * step + 1).wait()
        first, second = dests_ref[2 * step], dests_ref[2 * step + 1]
        degree = jnp.where(row < deg_block, first * deg_block + row, (second - 1) * deg_block + row)
        for j in range(per):
            order = ids_ref[half * per + j]
            used = (first // 2 + 1) * span > order

            @pl.when(used)
            def _():
                here = slice(step * span, (step + 1) * span)
                product = lax.dot_general(leg[j, here, :], spectra[j], NT, preferred_element_type=jnp.float32)
                product = jnp.where(degree >= order, product, 0.0)
                for d in range(2):
                    own = product[d * deg_block:(d + 1) * deg_block]
                    for c in range(2):
                        at = (2 * j + c) * deg_block
                        send[2 * step + d, at:at + deg_block, :] = own[:, c * 128:(c + 1) * 128].astype(jnp.bfloat16)
                rest[j, :, 0:16] = product[:, 256:]

            @pl.when(jnp.logical_not(used))
            def _():
                for d in range(2):
                    at = 2 * j * deg_block
                    send[2 * step + d, at:at + 2 * deg_block, :] = jnp.zeros((2 * deg_block, 128), jnp.bfloat16)
                rest[j, :, 0:16] = jnp.zeros((span, 16), jnp.float32)

        tail = jnp.concatenate([rest[j, :, 0:16] for j in range(per)], axis=1)
        for d in range(2):
            packed = jnp.concatenate([
                tail[d * deg_block + g * chunk:d * deg_block + (g + 1) * chunk] for g in range(groups)], axis=1)
            at = pairs * deg_block
            send[2 * step + d, at:at + chunk, :] = packed.astype(jnp.bfloat16)
            k = 2 * step + d
            pltpu.make_async_copy(send.at[k], outs[k], out_sems.at[k]).start()
    for k in range(count):
        pltpu.make_async_copy(send.at[k], outs[k], out_sems.at[k]).wait()


def legendre_sums(own_orders, dests, arrived, legendre, per, half, lev_dev, cycles_dev):
    _, degrees, cycles = legendre.shape
    ord_count, lev_count = arrived.shape[:2]
    deg_block = degrees // lev_count
    packed = 2 * per * deg_block + tail_rows(deg_block, per)
    kernel = functools.partial(legendre_kernel, lev_dev=lev_dev, cycles_dev=cycles_dev, deg_block=deg_block, half=half)
    anywhere = pl.BlockSpec(memory_space=pl.ANY)
    return pl.pallas_call(
        kernel,
        grid_spec=pltpu.PrefetchScalarGridSpec(
            num_scalar_prefetch=2,
            grid=(),
            in_specs=[anywhere] * 2,
            out_specs=[anywhere] * lev_count,
            scratch_shapes=[
                pltpu.VMEM(arrived.shape, jnp.bfloat16),
                pltpu.VMEM((per, degrees, cycles), jnp.bfloat16),
                pltpu.VMEM((cycles // 128, 2 * per * lev_count * lev_dev, 128), jnp.float32),
                pltpu.VMEM((per, 2 * lev_count * lev_dev, cycles), jnp.bfloat16),
                pltpu.VMEM((per, 2 * deg_block, 128), jnp.float32),
                pltpu.VMEM((lev_count, packed, 128), jnp.bfloat16),
                pltpu.SemaphoreType.DMA((lev_count,)),
                pltpu.SemaphoreType.DMA((lev_count,)),
                pltpu.SemaphoreType.DMA((lev_count,)),
            ],
        ),
        out_shape=[jax.ShapeDtypeStruct((packed, 128), jnp.bfloat16)] * lev_count,
        compiler_params=pltpu.CompilerParams(vmem_limit_bytes=FULL),
        cost_estimate=pl.CostEstimate(flops=3 * 10**9, bytes_accessed=20 * MIB, transcendentals=0),
        name="legendre_sums",
    )(own_orders, dests, arrived, legendre)


def degrees_first_kernel(cov_ref, out_ref, tail_ref, front, back):
    step = pl.program_id(0)
    group, levels, deg_block = cov_ref.shape
    last = pl.num_programs(0) - 1

    @pl.when(step < last)
    def _():
        for g in range(group):
            block = cov_ref[g].astype(jnp.float32)
            at = pl.ds(step * group + g, deg_block, stride=levels)
            front[at, :] = block[:128].T
            back[at, :] = jnp.concatenate([block[128:], jnp.zeros((120, deg_block), jnp.float32)], axis=0).T

    @pl.when(step == last)
    def _():
        def narrow(n, carry):
            rows = pl.ds(pl.multiple_of(n * levels, 8), levels)
            out_ref[n, 0:levels, :] = front[rows, :].astype(jnp.bfloat16)
            return carry

        lax.fori_loop(0, deg_block, narrow, 0, unroll=4)

        def pack(g, carry):
            total = back[pl.ds(pl.multiple_of(g * 16 * levels, 8), levels), :]
            for i in range(1, 16):
                rows = pl.ds(pl.multiple_of((g * 16 + i) * levels, 8), levels)
                total = total + pltpu.roll(back[rows, :], 8 * i, 1)
            tail_ref[g, 0:levels, :] = total.astype(jnp.bfloat16)
            return carry

        lax.fori_loop(0, deg_block // 16, pack, 0)


def degrees_first(cov_levels):
    levels, _, deg_block = cov_levels.shape
    group = 17
    steps = levels // group
    padded = -(-levels // 16) * 16
    return pl.pallas_call(
        degrees_first_kernel,
        grid=(steps + 1,),
        in_specs=[pl.BlockSpec((group, levels, deg_block), lambda s: (jnp.minimum(s, steps - 1), 0, 0))],
        out_specs=[
            pl.BlockSpec((deg_block, padded, 128), lambda s: (0, 0, 0), pipeline_mode=pl.Buffered(1)),
            pl.BlockSpec((deg_block // 16, padded, 128), lambda s: (0, 0, 0), pipeline_mode=pl.Buffered(1)),
        ],
        out_shape=[
            jax.ShapeDtypeStruct((deg_block, padded, 128), jnp.bfloat16),
            jax.ShapeDtypeStruct((deg_block // 16, padded, 128), jnp.bfloat16),
        ],
        scratch_shapes=[pltpu.VMEM((deg_block * levels, 128), jnp.float32)] * 2,
        compiler_params=pltpu.CompilerParams(vmem_limit_bytes=FULL),
        cost_estimate=pl.CostEstimate(flops=10**9, bytes_accessed=3 * 10**7, transcendentals=0),
        name="degrees_first",
    )(cov_levels)


def covariance_kernel(place_ref, *refs, per, count, carried):
    got_hbm, cov_hbm, tail_hbm = refs[:count], refs[count], refs[count + 1]
    out_ref, gots, cov, cov_tail, main, rest, out_main, out_rest, got_sems, cov_sems, tail_sem = refs[count + 2 + carried:]
    step = pl.program_id(0)
    deg_block, levels = out_ref.shape[3], out_ref.shape[2]
    pairs = 2 * per
    groups = 128 // (8 * pairs)
    chunk = deg_block // groups
    rows = count * pairs
    pitch = main.shape[0] // rows
    pieces = cov_sems.shape[0]
    piece = deg_block // pieces

    def load_got(s):
        return pltpu.make_async_copy(got_hbm[s], gots.at[s], got_sems.at[s])

    def load_cov(p):
        part = pl.ds(p * piece, piece)
        return pltpu.make_async_copy(cov_hbm.at[part], cov.at[part], cov_sems.at[p])

    @pl.when(step == 0)
    def _():
        for s in range(count):
            load_got(s).start()
        load_tail = pltpu.make_async_copy(tail_hbm, cov_tail, tail_sem)
        load_tail.start()
        for p in range(4):
            load_cov(p).start()
        for s in range(count):
            load_got(s).wait()
            at = pairs * deg_block
            tail = gots[s, at:at + chunk, :].astype(jnp.float32)
            for r in range(pairs):
                base = (s * pairs + r) * pitch
                main[base:base + deg_block, :] = gots[s, r * deg_block:(r + 1) * deg_block, :].astype(jnp.float32)
                for g in range(groups):
                    lane = (g * pairs + r) * 8
                    moved = tail if lane == 0 else pltpu.roll(tail, 128 - lane, 1)
                    rest[base + g * chunk:base + (g + 1) * chunk, :] = moved

        load_tail.wait()

        def share(p, carry):
            load_cov(p).wait()

            @pl.when(p + 4 < pieces)
            def _():
                load_cov(p + 4).start()

            for i in range(piece):
                n = p * piece + i
                left = jnp.concatenate([
                    main[pl.ds(n, rows, stride=pitch), :],
                    rest[pl.ds(n, rows, stride=pitch), :]], axis=1)[:, :levels].astype(jnp.bfloat16)
                right = jnp.concatenate([cov[n, 0:levels, :], cov_tail[p, 0:levels, :]], axis=1)
                product = jnp.dot(left, right, preferred_element_type=jnp.float32)
                out_main[pl.ds(n, rows, stride=pitch), :] = product[:, :128]
                last = product[:, 128:]
                out_rest[pl.ds(n, rows, stride=pitch), :] = last if i == 0 else pltpu.roll(last, 128 - 8 * i, 1)
            return carry

        lax.fori_loop(0, pieces, share, 0)

    for r in range(pairs):
        base = pl.multiple_of((step * pairs + r) * pitch, 8)
        out_ref[r // 2, r % 2, 0:128, :] = out_main[pl.ds(base, deg_block), :].T
        out_ref[r // 2, r % 2, 128:, :] = out_rest[pl.ds(base, deg_block), :][:, :levels - 128].T


def covariance(places, arrived, cov, cov_tail, out, orders, levels, per, half, halves):
    count = len(arrived)
    deg_block = cov.shape[0]
    rows = count * 2 * per * (deg_block + 8)
    carried = 0 if out is None else 1
    anywhere = pl.BlockSpec(memory_space=pl.ANY)
    return pl.pallas_call(
        functools.partial(covariance_kernel, per=per, count=count, carried=carried),
        grid_spec=pltpu.PrefetchScalarGridSpec(
            num_scalar_prefetch=1,
            grid=(count,),
            in_specs=[anywhere] * (count + 2 + carried),
            out_specs=pl.BlockSpec((per, 2, levels, deg_block), lambda s, place: (place[s] * halves + half, 0, 0, 0)),
            scratch_shapes=[
                pltpu.VMEM((count,) + arrived[0].shape, jnp.bfloat16),
                pltpu.VMEM(cov.shape, jnp.bfloat16),
                pltpu.VMEM(cov_tail.shape, jnp.bfloat16),
            ] + [pltpu.VMEM((rows, 128), jnp.float32)] * 4 + [
                pltpu.SemaphoreType.DMA((count,)),
                pltpu.SemaphoreType.DMA((deg_block // 16,)),
                pltpu.SemaphoreType.DMA,
            ],
        ),
        out_shape=jax.ShapeDtypeStruct((orders, 2, levels, deg_block), jnp.float32),
        input_output_aliases={count + 3: 0} if carried else {},
        compiler_params=pltpu.CompilerParams(vmem_limit_bytes=FULL),
        cost_estimate=pl.CostEstimate(flops=2 * 10**9, bytes_accessed=16 * MIB, transcendentals=0),
        name="vertical_covariance",
    )(places, *arrived, cov, cov_tail, *([out] if carried else []))


HALVES = 1


def shards(grid_grad, legendre, cov_root, order_ids, cycle_map):
    cycles_dev, lev_dev, lon_count = grid_grad.shape
    orders_dev, degree_count, cycle_total = legendre.shape
    ord_count = lax.axis_size("ord")
    lev_count = lax.axis_size("lev")
    dests = ord_count * lev_count
    chips = lev_count // 2
    per = orders_dev // HALVES
    lev = lax.axis_index("lev")
    position = lax.axis_index("ord") * lev_count + lev
    own_orders = lax.dynamic_slice_in_dim(order_ids, position * orders_dev, orders_dev, 0)
    grid_rows = grid_grad.transpose(1, 0, 2).reshape(lev_dev * cycles_dev, lon_count)

    near = [(d, f) for d in (1, chips - 1) for f in (0, 1)]
    far = [(d, f) for d in range(2, chips - 1) for f in (0, 1)]
    home = [(0, 1), (0, 0)]
    moves = near + far + home

    def moved(rank, d, f):
        return (rank // 2 + d) % chips * 2 + (rank % 2 + f) % 2

    targets = jnp.stack([moved(lev, d, f) for d, f in moves]).astype(jnp.int32)

    spectra = [fourier(grid_rows, order_ids, dests, per, 0)]
    spectra[0], cycle_map, cov_root = lax.optimization_barrier((spectra[0], cycle_map, cov_root))
    arranged = arrange_legendre(own_orders, cycle_map, legendre, 2 * degree_count // lev_count)
    cov, cov_tail = degrees_first(cov_root.transpose(1, 2, 0))
    arranged, cov, cov_tail = lax.optimization_barrier((arranged, cov, cov_tail))
    blocks = lax.all_to_all(spectra[0], ("ord", "lev"), split_axis=0, concat_axis=0, tiled=True)
    blocks = blocks.reshape((ord_count, lev_count) + blocks.shape[1:])
    packed = legendre_sums(own_orders, targets, blocks, arranged, per, 0, lev_dev, cycles_dev)
    sent = dict(zip(moves, packed))
    got = {(0, 0): sent[0, 0]}

    def exchange(some):
        for d, f in some:
            pairs = [(rank, moved(rank, d, f)) for rank in range(lev_count)]
            got[d, f] = lax.ppermute(sent[d, f], "lev", pairs)

    def apply(some, out):
        places = jnp.stack([moved(lev, chips - d, f) for d, f in some]).astype(jnp.int32)
        return covariance(places, [got[m] for m in some], cov, cov_tail, out, orders_dev * lev_count, lev_dev * lev_count, per, 0, HALVES)

    exchange(near + home[:1])
    out = apply(home, None)
    tied, out = lax.optimization_barrier(([got[m] for m in near] + [sent[m] for m in far], out))
    for m, block in zip(near + far, tied):
        (got if m in near else sent)[m] = block
    exchange(far)
    out = apply(near, out)
    out = apply(far, out)
    return out.transpose(3, 0, 1, 2)


def solution(mesh):
    return jax.shard_map(
        shards,
        mesh=mesh,
        in_specs=(
            P("ord", "lev", None),
            P(("ord", "lev"), None, None),
            P("lev", None, None),
            P(),
            P(),
        ),
        out_specs=P("lev", "ord", None, None),
        check_vma=False,
    )
```

```python
import functools
import math

import jax
import jax.numpy as jnp
from jax import lax
from jax.experimental import pallas as pl
from jax.experimental.pallas import tpu as pltpu
from jax.sharding import PartitionSpec as P

MIB = 1024 * 1024
FULL = 62 * MIB
NT = (((1,), (1,)), ((), ()))


def cosine(phase, lon_count):
    turns = jnp.floor(phase * (1.0 / lon_count) + 0.5)
    folded = jnp.abs(phase - turns * lon_count)
    angle = (lon_count / 4 - folded) * (2.0 * math.pi / lon_count)
    square = angle * angle
    series = -1.0 / 39916800
    for factor in (1.0 / 362880, -1.0 / 5040, 1.0 / 120, -1.0 / 6, 1.0):
        series = series * square + factor
    return series * angle


def fourier_kernel(ids_ref, grid_hbm, out_ref, table, field, sem, *, orders_dev, per, half):
    step = pl.program_id(0)
    rows, lon_count = table.shape
    blocks = lon_count // 128
    middle = blocks // 2
    group = 16

    @pl.when(step == 0)
    def _():
        load = pltpu.make_async_copy(grid_hbm, field, sem)
        load.start()
        row = lax.broadcasted_iota(jnp.int32, (group, 128), 0)
        lane = lax.broadcasted_iota(jnp.int32, (group, 128), 1).astype(jnp.float32)
        offset = jnp.where((row & 1) == 1, lon_count // 4, 0).astype(jnp.float32)

        def fill(g, carry):
            start = pl.multiple_of(g * group, group)
            order = jnp.zeros((group, 128), jnp.int32)
            for i in range(group // 2):
                k = g * (group // 2) + i
                order = jnp.where(row // 2 == i, ids_ref[k // per * orders_dev + half * per + k % per], order)
            order = order.astype(jnp.float32)
            scale = jnp.where(order == 0.0, 1.0, 2.0)
            double = 2.0 * cosine(order * 128.0, lon_count)
            below = scale * cosine(order * (lane + (middle - 1) * 128.0) + offset, lon_count)
            above = scale * cosine(order * (lane + middle * 128.0) + offset, lon_count)
            for a, first, second in ((middle - 1, above, below), (middle, below, above)):
                ahead = 1 if a == middle else -1
                while 0 <= a < blocks:
                    table[pl.ds(start, group), a * 128:(a + 1) * 128] = second.astype(jnp.bfloat16)
                    first, second = second, double * second - first
                    a += ahead
            return carry

        lax.fori_loop(0, rows // group, fill, 0, unroll=4)
        load.wait()

    share = rows // pl.num_programs(0)
    mine = pl.ds(pl.multiple_of(step * share, 16), share)
    spectra = lax.dot_general(table[mine, :], field[...], NT, preferred_element_type=jnp.float32)
    out_ref[...] = spectra.reshape(out_ref.shape).astype(jnp.bfloat16)


def fourier(grid_rows, order_ids, dests, per, half):
    points, lon_count = grid_rows.shape
    orders_dev = order_ids.shape[0] // dests
    rows = 2 * dests * per
    steps = per
    kernel = functools.partial(fourier_kernel, orders_dev=orders_dev, per=per, half=half)
    return pl.pallas_call(
        kernel,
        grid_spec=pltpu.PrefetchScalarGridSpec(
            num_scalar_prefetch=1,
            grid=(steps,),
            in_specs=[pl.BlockSpec(memory_space=pl.ANY)],
            out_specs=pl.BlockSpec((dests // steps, 2 * per, points), lambda s, ids: (s, 0, 0)),
            scratch_shapes=[
                pltpu.VMEM((rows, lon_count), jnp.bfloat16),
                pltpu.VMEM((points, lon_count), jnp.bfloat16),
                pltpu.SemaphoreType.DMA,
            ],
        ),
        out_shape=jax.ShapeDtypeStruct((dests, 2 * per, points), jnp.bfloat16),
        compiler_params=pltpu.CompilerParams(vmem_limit_bytes=FULL),
        cost_estimate=pl.CostEstimate(flops=2 * rows * points * lon_count, bytes_accessed=10 * MIB, transcendentals=0),
        name="fourier_analysis",
    )(order_ids, grid_rows)


def arrange_kernel(ids_ref, map_ref, leg_ref, out_ref, pick):
    j, step = pl.program_id(0), pl.program_id(1)
    span, cycles = leg_ref.shape[1:]

    @pl.when((j == 0) & (step == 0))
    def _():
        for r in range(0, cycles, 128):
            cycle = r + lax.broadcasted_iota(jnp.int32, (128, cycles), 0)
            pick[r:r + 128, :] = jnp.where(cycle == map_ref[...], 1.0, 0.0).astype(jnp.bfloat16)

    @pl.when((step + 1) * span > ids_ref[j])
    def _():
        out_ref[0] = jnp.dot(leg_ref[0], pick[...], preferred_element_type=jnp.float32).astype(jnp.bfloat16)


def arrange_legendre(own_orders, cycle_map, legendre, span):
    orders, degrees, cycles = legendre.shape
    return pl.pallas_call(
        arrange_kernel,
        grid_spec=pltpu.PrefetchScalarGridSpec(
            num_scalar_prefetch=1,
            grid=(orders, degrees // span),
            in_specs=[
                pl.BlockSpec((1, cycles), lambda j, s, ids: (0, 0)),
                pl.BlockSpec((1, span, cycles), lambda j, s, ids: (j, jnp.maximum(s, ids[j] // span), 0)),
            ],
            out_specs=pl.BlockSpec((1, span, cycles), lambda j, s, ids: (j, jnp.maximum(s, ids[j] // span), 0)),
            scratch_shapes=[pltpu.VMEM((cycles, cycles), jnp.bfloat16)],
        ),
        out_shape=jax.ShapeDtypeStruct(legendre.shape, jnp.bfloat16),
        compiler_params=pltpu.CompilerParams(vmem_limit_bytes=FULL),
        cost_estimate=pl.CostEstimate(
            flops=2 * orders * degrees * cycles * cycles, bytes_accessed=4 * orders * degrees * cycles, transcendentals=0),
        name="arrange_legendre",
    )(own_orders, cycle_map[None, :], legendre)


def tail_rows(deg_block, per):
    return -(-deg_block * 16 * per // 128 // 16) * 16


def legendre_kernel(ids_ref, dests_ref, got_hbm, leg_hbm, *refs, lev_dev, cycles_dev, deg_block, half):
    count = dests_ref.shape[0]
    outs = refs[:count]
    got, leg, rows_z, spectra, rest, send, got_sems, leg_sems, out_sems = refs[count:]
    ord_count, lev_count = got.shape[:2]
    per = leg.shape[0]
    pairs = 2 * per
    levels = lev_count * lev_dev
    span = 2 * deg_block
    steps = count // 2

    def load_got(b):
        return pltpu.make_async_copy(got_hbm.at[:, b], got.at[:, b], got_sems.at[b])

    def load_leg(k):
        source = leg_hbm.at[pl.ds(half * per, per), pl.ds(pl.multiple_of(dests_ref[k] * deg_block, 16), deg_block), :]
        return pltpu.make_async_copy(source, leg.at[:, pl.ds(k * deg_block, deg_block), :], leg_sems.at[k])

    for b in range(lev_count):
        load_got(b).start()
    def gather(b, carry):
        load_got(b).wait()
        load_leg(b).start()
        for l in range(lev_dev):
            row = jnp.concatenate([
                got[a, b, :, l * cycles_dev:(l + 1) * cycles_dev].astype(jnp.float32) for a in range(ord_count)
            ], axis=1)
            for t in range(rows_z.shape[0]):
                rows_z[t, pl.ds(b * lev_dev + l, pairs, stride=levels), :] = row[:, t * 128:(t + 1) * 128]
        return carry

    lax.fori_loop(0, lev_count, gather, 0)
    for j in range(per):
        for t in range(rows_z.shape[0]):
            lanes = slice(t * 128, (t + 1) * 128)
            tails = []
            for c in range(2):
                base = (2 * j + c) * levels
                spectra[j, c * 128:(c + 1) * 128, lanes] = rows_z[t, base:base + 128, :].astype(jnp.bfloat16)
                tails.append(rows_z[t, base + 128:base + levels, :])
            spectra[j, 256:, lanes] = jnp.concatenate(tails, axis=0).astype(jnp.bfloat16)

    row = lax.broadcasted_iota(jnp.int32, (span, 1), 0)
    groups = 128 // (16 * per)
    chunk = deg_block // groups
    for step in range(steps):
        load_leg(2 * step).wait()
        load_leg(2 * step + 1).wait()
        first, second = dests_ref[2 * step], dests_ref[2 * step + 1]
        degree = jnp.where(row < deg_block, first * deg_block + row, (second - 1) * deg_block + row)
        for j in range(per):
            order = ids_ref[half * per + j]
            used = (first // 2 + 1) * span > order

            @pl.when(used)
            def _():
                here = slice(step * span, (step + 1) * span)
                product = lax.dot_general(leg[j, here, :], spectra[j], NT, preferred_element_type=jnp.float32)
                product = jnp.where(degree >= order, product, 0.0)
                for d in range(2):
                    own = product[d * deg_block:(d + 1) * deg_block]
                    for c in range(2):
                        at = (2 * j + c) * deg_block
                        send[2 * step + d, at:at + deg_block, :] = own[:, c * 128:(c + 1) * 128].astype(jnp.bfloat16)
                rest[j, :, 0:16] = product[:, 256:]

            @pl.when(jnp.logical_not(used))
            def _():
                for d in range(2):
                    at = 2 * j * deg_block
                    send[2 * step + d, at:at + 2 * deg_block, :] = jnp.zeros((2 * deg_block, 128), jnp.bfloat16)
                rest[j, :, 0:16] = jnp.zeros((span, 16), jnp.float32)

        tail = jnp.concatenate([rest[j, :, 0:16] for j in range(per)], axis=1)
        for d in range(2):
            packed = jnp.concatenate([
                tail[d * deg_block + g * chunk:d * deg_block + (g + 1) * chunk] for g in range(groups)], axis=1)
            at = pairs * deg_block
            send[2 * step + d, at:at + chunk, :] = packed.astype(jnp.bfloat16)
            k = 2 * step + d
            pltpu.make_async_copy(send.at[k], outs[k], out_sems.at[k]).start()
    for k in range(count):
        pltpu.make_async_copy(send.at[k], outs[k], out_sems.at[k]).wait()


def legendre_sums(own_orders, dests, arrived, legendre, per, half, lev_dev, cycles_dev):
    _, degrees, cycles = legendre.shape
    ord_count, lev_count = arrived.shape[:2]
    deg_block = degrees // lev_count
    packed = 2 * per * deg_block + tail_rows(deg_block, per)
    kernel = functools.partial(legendre_kernel, lev_dev=lev_dev, cycles_dev=cycles_dev, deg_block=deg_block, half=half)
    anywhere = pl.BlockSpec(memory_space=pl.ANY)
    return pl.pallas_call(
        kernel,
        grid_spec=pltpu.PrefetchScalarGridSpec(
            num_scalar_prefetch=2,
            grid=(),
            in_specs=[anywhere] * 2,
            out_specs=[anywhere] * lev_count,
            scratch_shapes=[
                pltpu.VMEM(arrived.shape, jnp.bfloat16),
                pltpu.VMEM((per, degrees, cycles), jnp.bfloat16),
                pltpu.VMEM((cycles // 128, 2 * per * lev_count * lev_dev, 128), jnp.float32),
                pltpu.VMEM((per, 2 * lev_count * lev_dev, cycles), jnp.bfloat16),
                pltpu.VMEM((per, 2 * deg_block, 128), jnp.float32),
                pltpu.VMEM((lev_count, packed, 128), jnp.bfloat16),
                pltpu.SemaphoreType.DMA((lev_count,)),
                pltpu.SemaphoreType.DMA((lev_count,)),
                pltpu.SemaphoreType.DMA((lev_count,)),
            ],
        ),
        out_shape=[jax.ShapeDtypeStruct((packed, 128), jnp.bfloat16)] * lev_count,
        compiler_params=pltpu.CompilerParams(vmem_limit_bytes=FULL),
        cost_estimate=pl.CostEstimate(flops=3 * 10**9, bytes_accessed=20 * MIB, transcendentals=0),
        name="legendre_sums",
    )(own_orders, dests, arrived, legendre)


def degrees_first_kernel(cov_ref, out_ref, tail_ref, front, back):
    step = pl.program_id(0)
    group, levels, deg_block = cov_ref.shape
    last = pl.num_programs(0) - 1

    @pl.when(step < last)
    def _():
        for g in range(group):
            block = cov_ref[g].astype(jnp.float32)
            at = pl.ds(step * group + g, deg_block, stride=levels)
            front[at, :] = block[:128].T
            back[at, :] = jnp.concatenate([block[128:], jnp.zeros((120, deg_block), jnp.float32)], axis=0).T

    @pl.when(step == last)
    def _():
        def narrow(n, carry):
            rows = pl.ds(pl.multiple_of(n * levels, 8), levels)
            out_ref[n, 0:levels, :] = front[rows, :].astype(jnp.bfloat16)
            return carry

        lax.fori_loop(0, deg_block, narrow, 0, unroll=4)

        def pack(g, carry):
            total = back[pl.ds(pl.multiple_of(g * 16 * levels, 8), levels), :]
            for i in range(1, 16):
                rows = pl.ds(pl.multiple_of((g * 16 + i) * levels, 8), levels)
                total = total + pltpu.roll(back[rows, :], 8 * i, 1)
            tail_ref[g, 0:levels, :] = total.astype(jnp.bfloat16)
            return carry

        lax.fori_loop(0, deg_block // 16, pack, 0)


def degrees_first(cov_levels):
    levels, _, deg_block = cov_levels.shape
    group = 17
    steps = levels // group
    padded = -(-levels // 16) * 16
    return pl.pallas_call(
        degrees_first_kernel,
        grid=(steps + 1,),
        in_specs=[pl.BlockSpec((group, levels, deg_block), lambda s: (jnp.minimum(s, steps - 1), 0, 0))],
        out_specs=[
            pl.BlockSpec((deg_block, padded, 128), lambda s: (0, 0, 0), pipeline_mode=pl.Buffered(1)),
            pl.BlockSpec((deg_block // 16, padded, 128), lambda s: (0, 0, 0), pipeline_mode=pl.Buffered(1)),
        ],
        out_shape=[
            jax.ShapeDtypeStruct((deg_block, padded, 128), jnp.bfloat16),
            jax.ShapeDtypeStruct((deg_block // 16, padded, 128), jnp.bfloat16),
        ],
        scratch_shapes=[pltpu.VMEM((deg_block * levels, 128), jnp.float32)] * 2,
        compiler_params=pltpu.CompilerParams(vmem_limit_bytes=FULL),
        cost_estimate=pl.CostEstimate(flops=10**9, bytes_accessed=3 * 10**7, transcendentals=0),
        name="degrees_first",
    )(cov_levels)


def covariance_kernel(place_ref, *refs, per, count, carried):
    got_hbm, cov_hbm, tail_hbm = refs[:count], refs[count], refs[count + 1]
    out_ref, gots, cov, cov_tail, main, rest, out_main, out_rest, got_sems, cov_sems, tail_sem = refs[count + 2 + carried:]
    step = pl.program_id(0)
    deg_block, levels = out_ref.shape[3], out_ref.shape[2]
    pairs = 2 * per
    groups = 128 // (8 * pairs)
    chunk = deg_block // groups
    rows = count * pairs
    pitch = main.shape[0] // rows
    pieces = cov_sems.shape[0]
    piece = deg_block // pieces

    def load_got(s):
        return pltpu.make_async_copy(got_hbm[s], gots.at[s], got_sems.at[s])

    def load_cov(p):
        part = pl.ds(p * piece, piece)
        return pltpu.make_async_copy(cov_hbm.at[part], cov.at[part], cov_sems.at[p])

    @pl.when(step == 0)
    def _():
        for s in range(count):
            load_got(s).start()
        load_tail = pltpu.make_async_copy(tail_hbm, cov_tail, tail_sem)
        load_tail.start()
        for p in range(4):
            load_cov(p).start()
        for s in range(count):
            load_got(s).wait()
            at = pairs * deg_block
            tail = gots[s, at:at + chunk, :].astype(jnp.float32)
            for r in range(pairs):
                base = (s * pairs + r) * pitch
                main[base:base + deg_block, :] = gots[s, r * deg_block:(r + 1) * deg_block, :].astype(jnp.float32)
                for g in range(groups):
                    lane = (g * pairs + r) * 8
                    moved = tail if lane == 0 else pltpu.roll(tail, 128 - lane, 1)
                    rest[base + g * chunk:base + (g + 1) * chunk, :] = moved

        load_tail.wait()

        def share(p, carry):
            load_cov(p).wait()

            @pl.when(p + 4 < pieces)
            def _():
                load_cov(p + 4).start()

            for i in range(piece):
                n = p * piece + i
                left = jnp.concatenate([
                    main[pl.ds(n, rows, stride=pitch), :],
                    rest[pl.ds(n, rows, stride=pitch), :]], axis=1)[:, :levels].astype(jnp.bfloat16)
                right = jnp.concatenate([cov[n, 0:levels, :], cov_tail[p, 0:levels, :]], axis=1)
                product = jnp.dot(left, right, preferred_element_type=jnp.float32)
                out_main[pl.ds(n, rows, stride=pitch), :] = product[:, :128]
                last = product[:, 128:]
                out_rest[pl.ds(n, rows, stride=pitch), :] = last if i == 0 else pltpu.roll(last, 128 - 8 * i, 1)
            return carry

        lax.fori_loop(0, pieces, share, 0)

    for r in range(pairs):
        base = pl.multiple_of((step * pairs + r) * pitch, 8)
        out_ref[r // 2, r % 2, 0:128, :] = out_main[pl.ds(base, deg_block), :].T
        out_ref[r // 2, r % 2, 128:, :] = out_rest[pl.ds(base, deg_block), :][:, :levels - 128].T


def covariance(places, first, arrived, cov, cov_tail, out, orders, levels, per, half, halves):
    count = len(arrived)
    deg_block = cov.shape[0]
    rows = count * 2 * per * (deg_block + 8)
    carried = 0 if out is None else 1
    anywhere = pl.BlockSpec(memory_space=pl.ANY)
    return pl.pallas_call(
        functools.partial(covariance_kernel, per=per, count=count, carried=carried),
        grid_spec=pltpu.PrefetchScalarGridSpec(
            num_scalar_prefetch=1,
            grid=(count,),
            in_specs=[anywhere] * (count + 2 + carried),
            out_specs=pl.BlockSpec((per, 2, levels, deg_block), lambda s, place: (place[first + s] * halves + half, 0, 0, 0)),
            scratch_shapes=[
                pltpu.VMEM((count,) + arrived[0].shape, jnp.bfloat16),
                pltpu.VMEM(cov.shape, jnp.bfloat16),
                pltpu.VMEM(cov_tail.shape, jnp.bfloat16),
            ] + [pltpu.VMEM((rows, 128), jnp.float32)] * 4 + [
                pltpu.SemaphoreType.DMA((count,)),
                pltpu.SemaphoreType.DMA((deg_block // 16,)),
                pltpu.SemaphoreType.DMA,
            ],
        ),
        out_shape=jax.ShapeDtypeStruct((orders, 2, levels, deg_block), jnp.float32),
        input_output_aliases={count + 3: 0} if carried else {},
        compiler_params=pltpu.CompilerParams(vmem_limit_bytes=FULL),
        cost_estimate=pl.CostEstimate(flops=2 * 10**9, bytes_accessed=16 * MIB, transcendentals=0),
        name="vertical_covariance",
    )(places, *arrived, cov, cov_tail, *([out] if carried else []))


HALVES = 1


def shards(grid_grad, legendre, cov_root, order_ids, cycle_map):
    cycles_dev, lev_dev, lon_count = grid_grad.shape
    orders_dev, degree_count, cycle_total = legendre.shape
    ord_count = lax.axis_size("ord")
    lev_count = lax.axis_size("lev")
    dests = ord_count * lev_count
    chips = lev_count // 2
    per = orders_dev // HALVES
    lev = lax.axis_index("lev")
    position = lax.axis_index("ord") * lev_count + lev
    own_orders = lax.dynamic_slice_in_dim(order_ids, position * orders_dev, orders_dev, 0)
    grid_rows = grid_grad.transpose(1, 0, 2).reshape(lev_dev * cycles_dev, lon_count)

    near = [(d, f) for d in (1, chips - 1) for f in (0, 1)]
    far = [(d, f) for d in range(2, chips - 1) for f in (0, 1)]
    home = [(0, 1), (0, 0)]
    moves = near + far + home

    def moved(rank, d, f):
        return (rank // 2 + d) % chips * 2 + (rank % 2 + f) % 2

    targets = jnp.stack([moved(lev, d, f) for d, f in moves]).astype(jnp.int32)

    spectra = [fourier(grid_rows, order_ids, dests, per, 0)]
    spectra[0], cycle_map, cov_root = lax.optimization_barrier((spectra[0], cycle_map, cov_root))
    arranged = arrange_legendre(own_orders, cycle_map, legendre, 2 * degree_count // lev_count)
    cov, cov_tail = degrees_first(cov_root.transpose(1, 2, 0))
    arranged, cov, cov_tail = lax.optimization_barrier((arranged, cov, cov_tail))
    blocks = lax.all_to_all(spectra[0], ("ord", "lev"), split_axis=0, concat_axis=0, tiled=True)
    blocks = blocks.reshape((ord_count, lev_count) + blocks.shape[1:])
    packed = legendre_sums(own_orders, targets, blocks, arranged, per, 0, lev_dev, cycles_dev)
    sent = dict(zip(moves, packed))
    got = {(0, 0): sent[0, 0]}

    def exchange(some):
        for d, f in some:
            pairs = [(rank, moved(rank, d, f)) for rank in range(lev_count)]
            got[d, f] = lax.ppermute(sent[d, f], "lev", pairs)

    turns = home + near + far
    places = jnp.stack([moved(lev, chips - d, f) for d, f in turns]).astype(jnp.int32)

    def apply(some, out):
        first = turns.index(some[0])
        return covariance(places, first, [got[m] for m in some], cov, cov_tail, out, orders_dev * lev_count, lev_dev * lev_count, per, 0, HALVES)

    exchange(near + home[:1])
    out = apply(home, None)
    ahead = near[:len(near) // 2]
    tied, out = lax.optimization_barrier(([got[m] for m in ahead] + [sent[m] for m in far], out))
    for m, block in zip(ahead + far, tied):
        (got if m in near else sent)[m] = block
    exchange(far)
    out = apply(near, out)
    out = apply(far, out)
    return out.transpose(3, 0, 1, 2)


def solution(mesh):
    return jax.shard_map(
        shards,
        mesh=mesh,
        in_specs=(
            P("ord", "lev", None),
            P(("ord", "lev"), None, None),
            P("lev", None, None),
            P(),
            P(),
        ),
        out_specs=P("lev", "ord", None, None),
        check_vma=False,
    )
```

```python
import functools
import math

import jax
import jax.numpy as jnp
from jax import lax
from jax.experimental import pallas as pl
from jax.experimental.pallas import tpu as pltpu
from jax.sharding import PartitionSpec as P

MIB = 1024 * 1024
FULL = 62 * MIB
NT = (((1,), (1,)), ((), ()))


def cosine(phase, lon_count):
    turns = jnp.floor(phase * (1.0 / lon_count) + 0.5)
    folded = jnp.abs(phase - turns * lon_count)
    angle = (lon_count / 4 - folded) * (2.0 * math.pi / lon_count)
    square = angle * angle
    series = -1.0 / 39916800
    for factor in (1.0 / 362880, -1.0 / 5040, 1.0 / 120, -1.0 / 6, 1.0):
        series = series * square + factor
    return series * angle


def fourier_kernel(ids_ref, grid_hbm, out_ref, table, field, sem, *, orders_dev, per, half):
    step = pl.program_id(0)
    rows, lon_count = table.shape
    blocks = lon_count // 128
    middle = blocks // 2
    group = 16

    @pl.when(step == 0)
    def _():
        load = pltpu.make_async_copy(grid_hbm, field, sem)
        load.start()
        row = lax.broadcasted_iota(jnp.int32, (group, 128), 0)
        lane = lax.broadcasted_iota(jnp.int32, (group, 128), 1).astype(jnp.float32)
        offset = jnp.where((row & 1) == 1, lon_count // 4, 0).astype(jnp.float32)

        def fill(g, carry):
            start = pl.multiple_of(g * group, group)
            order = jnp.zeros((group, 128), jnp.int32)
            for i in range(group // 2):
                k = g * (group // 2) + i
                order = jnp.where(row // 2 == i, ids_ref[k // per * orders_dev + half * per + k % per], order)
            order = order.astype(jnp.float32)
            scale = jnp.where(order == 0.0, 1.0, 2.0)
            double = 2.0 * cosine(order * 128.0, lon_count)
            below = scale * cosine(order * (lane + (middle - 1) * 128.0) + offset, lon_count)
            above = scale * cosine(order * (lane + middle * 128.0) + offset, lon_count)
            for a, first, second in ((middle - 1, above, below), (middle, below, above)):
                ahead = 1 if a == middle else -1
                while 0 <= a < blocks:
                    table[pl.ds(start, group), a * 128:(a + 1) * 128] = second.astype(jnp.bfloat16)
                    first, second = second, double * second - first
                    a += ahead
            return carry

        lax.fori_loop(0, rows // group, fill, 0, unroll=4)
        load.wait()

    share = rows // pl.num_programs(0)
    mine = pl.ds(pl.multiple_of(step * share, 16), share)
    spectra = lax.dot_general(table[mine, :], field[...], NT, preferred_element_type=jnp.float32)
    out_ref[...] = spectra.reshape(out_ref.shape).astype(jnp.bfloat16)


def fourier(grid_rows, order_ids, dests, per, half):
    points, lon_count = grid_rows.shape
    orders_dev = order_ids.shape[0] // dests
    rows = 2 * dests * per
    steps = per // 2
    kernel = functools.partial(fourier_kernel, orders_dev=orders_dev, per=per, half=half)
    return pl.pallas_call(
        kernel,
        grid_spec=pltpu.PrefetchScalarGridSpec(
            num_scalar_prefetch=1,
            grid=(steps,),
            in_specs=[pl.BlockSpec(memory_space=pl.ANY)],
            out_specs=pl.BlockSpec((dests // steps, 2 * per, points), lambda s, ids: (s, 0, 0)),
            scratch_shapes=[
                pltpu.VMEM((rows, lon_count), jnp.bfloat16),
                pltpu.VMEM((points, lon_count), jnp.bfloat16),
                pltpu.SemaphoreType.DMA,
            ],
        ),
        out_shape=jax.ShapeDtypeStruct((dests, 2 * per, points), jnp.bfloat16),
        compiler_params=pltpu.CompilerParams(vmem_limit_bytes=FULL),
        cost_estimate=pl.CostEstimate(flops=2 * rows * points * lon_count, bytes_accessed=10 * MIB, transcendentals=0),
        name="fourier_analysis",
    )(order_ids, grid_rows)


def arrange_kernel(ids_ref, map_ref, leg_ref, out_ref, pick):
    j, step = pl.program_id(0), pl.program_id(1)
    span, cycles = leg_ref.shape[1:]

    @pl.when((j == 0) & (step == 0))
    def _():
        for r in range(0, cycles, 128):
            cycle = r + lax.broadcasted_iota(jnp.int32, (128, cycles), 0)
            pick[r:r + 128, :] = jnp.where(cycle == map_ref[...], 1.0, 0.0).astype(jnp.bfloat16)

    @pl.when((step + 1) * span > ids_ref[j])
    def _():
        out_ref[0] = jnp.dot(leg_ref[0], pick[...], preferred_element_type=jnp.float32).astype(jnp.bfloat16)


def arrange_legendre(own_orders, cycle_map, legendre, span):
    orders, degrees, cycles = legendre.shape
    return pl.pallas_call(
        arrange_kernel,
        grid_spec=pltpu.PrefetchScalarGridSpec(
            num_scalar_prefetch=1,
            grid=(orders, degrees // span),
            in_specs=[
                pl.BlockSpec((1, cycles), lambda j, s, ids: (0, 0)),
                pl.BlockSpec((1, span, cycles), lambda j, s, ids: (j, jnp.maximum(s, ids[j] // span), 0)),
            ],
            out_specs=pl.BlockSpec((1, span, cycles), lambda j, s, ids: (j, jnp.maximum(s, ids[j] // span), 0)),
            scratch_shapes=[pltpu.VMEM((cycles, cycles), jnp.bfloat16)],
        ),
        out_shape=jax.ShapeDtypeStruct(legendre.shape, jnp.bfloat16),
        compiler_params=pltpu.CompilerParams(vmem_limit_bytes=FULL),
        cost_estimate=pl.CostEstimate(
            flops=2 * orders * degrees * cycles * cycles, bytes_accessed=4 * orders * degrees * cycles, transcendentals=0),
        name="arrange_legendre",
    )(own_orders, cycle_map[None, :], legendre)


def tail_rows(deg_block, per):
    return -(-deg_block * 16 * per // 128 // 16) * 16


def legendre_kernel(ids_ref, dests_ref, got_hbm, leg_hbm, *refs, lev_dev, cycles_dev, deg_block, half):
    count = dests_ref.shape[0]
    outs = refs[:count]
    got, leg, rows_z, spectra, rest, send, got_sems, leg_sems, out_sems = refs[count:]
    ord_count, lev_count = got.shape[:2]
    per = leg.shape[0]
    pairs = 2 * per
    levels = lev_count * lev_dev
    span = 2 * deg_block
    steps = count // 2

    def load_got(b):
        return pltpu.make_async_copy(got_hbm.at[:, b], got.at[:, b], got_sems.at[b])

    def load_leg(k):
        source = leg_hbm.at[pl.ds(half * per, per), pl.ds(pl.multiple_of(dests_ref[k] * deg_block, 16), deg_block), :]
        return pltpu.make_async_copy(source, leg.at[:, pl.ds(k * deg_block, deg_block), :], leg_sems.at[k])

    for b in range(lev_count):
        load_got(b).start()
    def gather(b, carry):
        load_got(b).wait()
        load_leg(b).start()
        for l in range(lev_dev):
            row = jnp.concatenate([
                got[a, b, :, l * cycles_dev:(l + 1) * cycles_dev].astype(jnp.float32) for a in range(ord_count)
            ], axis=1)
            for t in range(rows_z.shape[0]):
                rows_z[t, pl.ds(b * lev_dev + l, pairs, stride=levels), :] = row[:, t * 128:(t + 1) * 128]
        return carry

    lax.fori_loop(0, lev_count, gather, 0)
    for j in range(per):
        for t in range(rows_z.shape[0]):
            lanes = slice(t * 128, (t + 1) * 128)
            tails = []
            for c in range(2):
                base = (2 * j + c) * levels
                spectra[j, c * 128:(c + 1) * 128, lanes] = rows_z[t, base:base + 128, :].astype(jnp.bfloat16)
                tails.append(rows_z[t, base + 128:base + levels, :])
            spectra[j, 256:, lanes] = jnp.concatenate(tails, axis=0).astype(jnp.bfloat16)

    row = lax.broadcasted_iota(jnp.int32, (span, 1), 0)
    groups = 128 // (16 * per)
    chunk = deg_block // groups
    for step in range(steps):
        load_leg(2 * step).wait()
        load_leg(2 * step + 1).wait()
        first, second = dests_ref[2 * step], dests_ref[2 * step + 1]
        degree = jnp.where(row < deg_block, first * deg_block + row, (second - 1) * deg_block + row)
        for j in range(per):
            order = ids_ref[half * per + j]
            used = (first // 2 + 1) * span > order

            @pl.when(used)
            def _():
                here = slice(step * span, (step + 1) * span)
                product = lax.dot_general(leg[j, here, :], spectra[j], NT, preferred_element_type=jnp.float32)
                product = jnp.where(degree >= order, product, 0.0)
                for d in range(2):
                    own = product[d * deg_block:(d + 1) * deg_block]
                    for c in range(2):
                        at = (2 * j + c) * deg_block
                        send[2 * step + d, at:at + deg_block, :] = own[:, c * 128:(c + 1) * 128].astype(jnp.bfloat16)
                rest[j, :, 0:16] = product[:, 256:]

            @pl.when(jnp.logical_not(used))
            def _():
                for d in range(2):
                    at = 2 * j * deg_block
                    send[2 * step + d, at:at + 2 * deg_block, :] = jnp.zeros((2 * deg_block, 128), jnp.bfloat16)
                rest[j, :, 0:16] = jnp.zeros((span, 16), jnp.float32)

        tail = jnp.concatenate([rest[j, :, 0:16] for j in range(per)], axis=1)
        for d in range(2):
            packed = jnp.concatenate([
                tail[d * deg_block + g * chunk:d * deg_block + (g + 1) * chunk] for g in range(groups)], axis=1)
            at = pairs * deg_block
            send[2 * step + d, at:at + chunk, :] = packed.astype(jnp.bfloat16)
            k = 2 * step + d
            pltpu.make_async_copy(send.at[k], outs[k], out_sems.at[k]).start()
    for k in range(count):
        pltpu.make_async_copy(send.at[k], outs[k], out_sems.at[k]).wait()


def legendre_sums(own_orders, dests, arrived, legendre, per, half, lev_dev, cycles_dev):
    _, degrees, cycles = legendre.shape
    ord_count, lev_count = arrived.shape[:2]
    deg_block = degrees // lev_count
    packed = 2 * per * deg_block + tail_rows(deg_block, per)
    kernel = functools.partial(legendre_kernel, lev_dev=lev_dev, cycles_dev=cycles_dev, deg_block=deg_block, half=half)
    anywhere = pl.BlockSpec(memory_space=pl.ANY)
    return pl.pallas_call(
        kernel,
        grid_spec=pltpu.PrefetchScalarGridSpec(
            num_scalar_prefetch=2,
            grid=(),
            in_specs=[anywhere] * 2,
            out_specs=[anywhere] * lev_count,
            scratch_shapes=[
                pltpu.VMEM(arrived.shape, jnp.bfloat16),
                pltpu.VMEM((per, degrees, cycles), jnp.bfloat16),
                pltpu.VMEM((cycles // 128, 2 * per * lev_count * lev_dev, 128), jnp.float32),
                pltpu.VMEM((per, 2 * lev_count * lev_dev, cycles), jnp.bfloat16),
                pltpu.VMEM((per, 2 * deg_block, 128), jnp.float32),
                pltpu.VMEM((lev_count, packed, 128), jnp.bfloat16),
                pltpu.SemaphoreType.DMA((lev_count,)),
                pltpu.SemaphoreType.DMA((lev_count,)),
                pltpu.SemaphoreType.DMA((lev_count,)),
            ],
        ),
        out_shape=[jax.ShapeDtypeStruct((packed, 128), jnp.bfloat16)] * lev_count,
        compiler_params=pltpu.CompilerParams(vmem_limit_bytes=FULL),
        cost_estimate=pl.CostEstimate(flops=3 * 10**9, bytes_accessed=20 * MIB, transcendentals=0),
        name="legendre_sums",
    )(own_orders, dests, arrived, legendre)


def degrees_first_kernel(cov_ref, out_ref, tail_ref, front, back):
    step = pl.program_id(0)
    group, levels, deg_block = cov_ref.shape
    last = pl.num_programs(0) - 1

    @pl.when(step < last)
    def _():
        for g in range(group):
            block = cov_ref[g].astype(jnp.float32)
            at = pl.ds(step * group + g, deg_block, stride=levels)
            front[at, :] = block[:128].T
            back[at, :] = jnp.concatenate([block[128:], jnp.zeros((120, deg_block), jnp.float32)], axis=0).T

    @pl.when(step == last)
    def _():
        def narrow(n, carry):
            rows = pl.ds(pl.multiple_of(n * levels, 8), levels)
            out_ref[n, 0:levels, :] = front[rows, :].astype(jnp.bfloat16)
            return carry

        lax.fori_loop(0, deg_block, narrow, 0, unroll=4)

        def pack(g, carry):
            total = back[pl.ds(pl.multiple_of(g * 16 * levels, 8), levels), :]
            for i in range(1, 16):
                rows = pl.ds(pl.multiple_of((g * 16 + i) * levels, 8), levels)
                total = total + pltpu.roll(back[rows, :], 8 * i, 1)
            tail_ref[g, 0:levels, :] = total.astype(jnp.bfloat16)
            return carry

        lax.fori_loop(0, deg_block // 16, pack, 0)


def degrees_first(cov_levels):
    levels, _, deg_block = cov_levels.shape
    group = 17
    steps = levels // group
    padded = -(-levels // 16) * 16
    return pl.pallas_call(
        degrees_first_kernel,
        grid=(steps + 1,),
        in_specs=[pl.BlockSpec((group, levels, deg_block), lambda s: (jnp.minimum(s, steps - 1), 0, 0))],
        out_specs=[
            pl.BlockSpec((deg_block, padded, 128), lambda s: (0, 0, 0), pipeline_mode=pl.Buffered(1)),
            pl.BlockSpec((deg_block // 16, padded, 128), lambda s: (0, 0, 0), pipeline_mode=pl.Buffered(1)),
        ],
        out_shape=[
            jax.ShapeDtypeStruct((deg_block, padded, 128), jnp.bfloat16),
            jax.ShapeDtypeStruct((deg_block // 16, padded, 128), jnp.bfloat16),
        ],
        scratch_shapes=[pltpu.VMEM((deg_block * levels, 128), jnp.float32)] * 2,
        compiler_params=pltpu.CompilerParams(vmem_limit_bytes=FULL),
        cost_estimate=pl.CostEstimate(flops=10**9, bytes_accessed=3 * 10**7, transcendentals=0),
        name="degrees_first",
    )(cov_levels)


def covariance_kernel(place_ref, *refs, per, count, carried):
    got_hbm, cov_hbm, tail_hbm = refs[:count], refs[count], refs[count + 1]
    out_ref, gots, cov, cov_tail, main, rest, out_main, out_rest, got_sems, cov_sems, tail_sem = refs[count + 2 + carried:]
    step = pl.program_id(0)
    deg_block, levels = out_ref.shape[3], out_ref.shape[2]
    pairs = 2 * per
    groups = 128 // (8 * pairs)
    chunk = deg_block // groups
    rows = count * pairs
    pitch = main.shape[0] // rows
    pieces = cov_sems.shape[0]
    piece = deg_block // pieces

    def load_got(s):
        return pltpu.make_async_copy(got_hbm[s], gots.at[s], got_sems.at[s])

    def load_cov(p):
        part = pl.ds(p * piece, piece)
        return pltpu.make_async_copy(cov_hbm.at[part], cov.at[part], cov_sems.at[p])

    @pl.when(step == 0)
    def _():
        for s in range(count):
            load_got(s).start()
        load_tail = pltpu.make_async_copy(tail_hbm, cov_tail, tail_sem)
        load_tail.start()
        for p in range(4):
            load_cov(p).start()
        for s in range(count):
            load_got(s).wait()
            at = pairs * deg_block
            tail = gots[s, at:at + chunk, :].astype(jnp.float32)
            for r in range(pairs):
                base = (s * pairs + r) * pitch
                main[base:base + deg_block, :] = gots[s, r * deg_block:(r + 1) * deg_block, :].astype(jnp.float32)
                for g in range(groups):
                    lane = (g * pairs + r) * 8
                    moved = tail if lane == 0 else pltpu.roll(tail, 128 - lane, 1)
                    rest[base + g * chunk:base + (g + 1) * chunk, :] = moved

        load_tail.wait()

        def share(p, carry):
            load_cov(p).wait()

            @pl.when(p + 4 < pieces)
            def _():
                load_cov(p + 4).start()

            for i in range(piece):
                n = p * piece + i
                left = jnp.concatenate([
                    main[pl.ds(n, rows, stride=pitch), :],
                    rest[pl.ds(n, rows, stride=pitch), :]], axis=1)[:, :levels].astype(jnp.bfloat16)
                right = jnp.concatenate([cov[n, 0:levels, :], cov_tail[p, 0:levels, :]], axis=1)
                product = jnp.dot(left, right, preferred_element_type=jnp.float32)
                out_main[pl.ds(n, rows, stride=pitch), :] = product[:, :128]
                last = product[:, 128:]
                out_rest[pl.ds(n, rows, stride=pitch), :] = last if i == 0 else pltpu.roll(last, 128 - 8 * i, 1)
            return carry

        lax.fori_loop(0, pieces, share, 0)

    for r in range(pairs):
        base = pl.multiple_of((step * pairs + r) * pitch, 8)
        out_ref[r // 2, r % 2, 0:128, :] = out_main[pl.ds(base, deg_block), :].T
        out_ref[r // 2, r % 2, 128:, :] = out_rest[pl.ds(base, deg_block), :][:, :levels - 128].T


def covariance(places, first, arrived, cov, cov_tail, out, orders, levels, per, half, halves):
    count = len(arrived)
    deg_block = cov.shape[0]
    rows = count * 2 * per * (deg_block + 8)
    carried = 0 if out is None else 1
    anywhere = pl.BlockSpec(memory_space=pl.ANY)
    return pl.pallas_call(
        functools.partial(covariance_kernel, per=per, count=count, carried=carried),
        grid_spec=pltpu.PrefetchScalarGridSpec(
            num_scalar_prefetch=1,
            grid=(count,),
            in_specs=[anywhere] * (count + 2 + carried),
            out_specs=pl.BlockSpec((per, 2, levels, deg_block), lambda s, place: (place[first + s] * halves + half, 0, 0, 0)),
            scratch_shapes=[
                pltpu.VMEM((count,) + arrived[0].shape, jnp.bfloat16),
                pltpu.VMEM(cov.shape, jnp.bfloat16),
                pltpu.VMEM(cov_tail.shape, jnp.bfloat16),
            ] + [pltpu.VMEM((rows, 128), jnp.float32)] * 4 + [
                pltpu.SemaphoreType.DMA((count,)),
                pltpu.SemaphoreType.DMA((deg_block // 16,)),
                pltpu.SemaphoreType.DMA,
            ],
        ),
        out_shape=jax.ShapeDtypeStruct((orders, 2, levels, deg_block), jnp.float32),
        input_output_aliases={count + 3: 0} if carried else {},
        compiler_params=pltpu.CompilerParams(vmem_limit_bytes=FULL),
        cost_estimate=pl.CostEstimate(flops=2 * 10**9, bytes_accessed=16 * MIB, transcendentals=0),
        name="vertical_covariance",
    )(places, *arrived, cov, cov_tail, *([out] if carried else []))


HALVES = 1


def shards(grid_grad, legendre, cov_root, order_ids, cycle_map):
    cycles_dev, lev_dev, lon_count = grid_grad.shape
    orders_dev, degree_count, cycle_total = legendre.shape
    ord_count = lax.axis_size("ord")
    lev_count = lax.axis_size("lev")
    dests = ord_count * lev_count
    chips = lev_count // 2
    per = orders_dev // HALVES
    lev = lax.axis_index("lev")
    position = lax.axis_index("ord") * lev_count + lev
    own_orders = lax.dynamic_slice_in_dim(order_ids, position * orders_dev, orders_dev, 0)
    grid_rows = grid_grad.transpose(1, 0, 2).reshape(lev_dev * cycles_dev, lon_count)

    near = [(d, f) for d in (1, chips - 1) for f in (0, 1)]
    far = [(d, f) for d in range(2, chips - 1) for f in (0, 1)]
    home = [(0, 1), (0, 0)]
    moves = near + far + home

    def moved(rank, d, f):
        return (rank // 2 + d) % chips * 2 + (rank % 2 + f) % 2

    targets = jnp.stack([moved(lev, d, f) for d, f in moves]).astype(jnp.int32)

    spectra = [fourier(grid_rows, order_ids, dests, per, 0)]
    spectra[0], cycle_map, cov_root = lax.optimization_barrier((spectra[0], cycle_map, cov_root))
    arranged = arrange_legendre(own_orders, cycle_map, legendre, 2 * degree_count // lev_count)
    cov, cov_tail = degrees_first(cov_root.transpose(1, 2, 0))
    arranged, cov, cov_tail = lax.optimization_barrier((arranged, cov, cov_tail))
    blocks = lax.all_to_all(spectra[0], ("ord", "lev"), split_axis=0, concat_axis=0, tiled=True)
    blocks = blocks.reshape((ord_count, lev_count) + blocks.shape[1:])
    packed = legendre_sums(own_orders, targets, blocks, arranged, per, 0, lev_dev, cycles_dev)
    sent = dict(zip(moves, packed))
    got = {(0, 0): sent[0, 0]}

    def exchange(some):
        for d, f in some:
            pairs = [(rank, moved(rank, d, f)) for rank in range(lev_count)]
            got[d, f] = lax.ppermute(sent[d, f], "lev", pairs)

    turns = home + near + far
    places = jnp.stack([moved(lev, chips - d, f) for d, f in turns]).astype(jnp.int32)

    def apply(some, out):
        first = turns.index(some[0])
        return covariance(places, first, [got[m] for m in some], cov, cov_tail, out, orders_dev * lev_count, lev_dev * lev_count, per, 0, HALVES)

    exchange(near + home[:1])
    out = apply(home, None)
    tied, out = lax.optimization_barrier(([got[m] for m in near] + [sent[m] for m in far], out))
    for m, block in zip(near + far, tied):
        (got if m in near else sent)[m] = block
    exchange(far)
    out = apply(near, out)
    out = apply(far, out)
    return out.transpose(3, 0, 1, 2)


def solution(mesh):
    return jax.shard_map(
        shards,
        mesh=mesh,
        in_specs=(
            P("ord", "lev", None),
            P(("ord", "lev"), None, None),
            P("lev", None, None),
            P(),
            P(),
        ),
        out_specs=P("lev", "ord", None, None),
        check_vma=False,
    )
```
